256 devices in a mesh: slab: 32 (over z, y_lo, core), sub: 8 (over x, y_hi).
Axes of the slice: x: 4, y: 4 (y_hi: 2, y_lo: 2; y = y_hi * 2 + y_lo), z: 8, core: 2. Of those that a mesh axis runs over, the one named last changes fastest.
Arguments:
- features: bfloat16 [262144, 128], P(('slab', 'sub')), may hold values from -6 to 6
- positions: float32 [3, 262144], P(None, ('slab', 'sub')), may hold values from 0 to 1, as said below
- atom_count: int32 [256], P(('slab', 'sub')), may hold values from 512 to 1024, as said below
- kgrid: int32 [3, 2048], replicated, may hold values from -6 to 6
- k_filter: float32 [2048, 128], replicated, may hold values from 0.1 to 1
- w_mix: float32 [128, 128], replicated, may hold values from -0.5 to 0.5
- w_recv: bfloat16 [128, 128], replicated, may hold values from -0.5 to 0.5
- w_send: bfloat16 [128, 128], replicated, may hold values from -0.5 to 0.5
- w_basis: bfloat16 [8, 128], replicated, may hold values from -2 to 2
- w_out: bfloat16 [128, 128], replicated, may hold values from -0.5 to 0.5
- edge_basis: bfloat16 [8, 8388608], P(None, ('slab', 'sub')), may hold values from -1 to 1
- senders: int32 [8388608], P(('slab', 'sub')), may hold values from 0 to 9215, as said below
Outputs:
- updated: float32 [262144, 128], P(('slab', 'sub'))
The draws below stay inside these ranges and needn't reach their ends.
Inputs may be any that keep to these rules, and one draw needn't show every extreme that they name: `atom_count`: one block has exactly 1024 live atoms; live atoms of a block are its first rows. senders[e] = (3 a + c) * 1024 + j with a, c in 0..2 and j below the atom_count of the block it names. Each atom of block (s, b) has positions[0] in [b / 8, (b + 1) / 8), positions[2] in [s / 32, (s + 1) / 32), positions[1] in [0, 1).
All inputs are finite; a program needn't handle non-finite values.
Results may differ from the reference program's by a relative error of at most 0.0021.
Values may be sent and summed in bfloat16 or wider, within the bound.
No kernel may reach another device: no remote copies, remote signals or barrier semaphores. Data moves between devices by JAX's collectives and lax.ppermute only.
A program may use at most 128 MiB of HBM per device.

```python
import math
import jax
import jax.numpy as jnp
from jax import lax

A_DEV = 1024
C = 128
K = 2048
DEG = 32
NB = 8
SLABS = 32
COLS = 8
BLOCKS = 256
ATOMS = 262144
EDGES = 8388608


def block_counts(key):
    key = jax.random.fold_in(key, 7)
    first_key, second_key = jax.random.split(key)
    counts = jax.random.randint(first_key, (SLABS * COLS,), A_DEV // 2, A_DEV + 1)
    full_block = jax.random.randint(second_key, (), 0, SLABS * COLS)
    return (jnp.where(jnp.arange(SLABS * COLS) == full_block, A_DEV, counts).astype(jnp.int32), full_block)


def draw_atom_count(key, part):
    counts, full_block = block_counts(key)
    return counts


def draw_senders(key, part):
    counts, full_block = block_counts(key)
    key = jax.random.fold_in(key, 2)
    first_key, second_key, third_key = jax.random.split(key, 3)
    edge_slot = jnp.arange(EDGES, dtype=jnp.int32)
    block_index = edge_slot // (A_DEV * DEG)
    slab_index = block_index // COLS
    column = block_index % COLS
    slab_step = jax.random.randint(first_key, (EDGES,), 0, 3)
    col_step = jax.random.randint(second_key, (EDGES,), 0, 3)
    source = (slab_index + slab_step - 1) % SLABS * COLS + (column + col_step - 1) % COLS
    atom_index = jax.random.randint(third_key, (EDGES,), 0, counts[source])
    values = ((slab_step * 3 + col_step) * A_DEV + atom_index).astype(jnp.int32)
    full_slab = full_block // COLS
    full_col = full_block % COLS
    target = (full_slab + SLABS - 1) % SLABS * COLS + (full_col + COLS - 1) % COLS
    first_slot = target * (A_DEV * DEG)
    values = jnp.where(edge_slot == first_slot, 9 * A_DEV - 1, values)
    values = jnp.where(edge_slot == first_slot + 1, 0, values)
    return values.astype(jnp.int32)


def draw_positions(key, part):
    key = jax.random.fold_in(key, 3)
    uniform_vals = jax.random.uniform(key, (3, ATOMS), jnp.float32)
    block_index = jnp.arange(ATOMS, dtype=jnp.int32) // A_DEV
    column = (block_index % COLS).astype(jnp.float32)
    slab_index = (block_index // COLS).astype(jnp.float32)
    first_dim = (column + uniform_vals[0]) / COLS
    third_dim = (slab_index + uniform_vals[2]) / SLABS
    return jnp.stack([first_dim, uniform_vals[1], third_dim], axis=0).astype(jnp.float32)


def set_ends(values, stream_key, smallest, top_value):
    shape = values.shape
    index_at = [jax.random.randint(jax.random.fold_in(stream_key, axis), (), 0, shape[axis]) for axis in range(len(shape))]
    values = values.at[tuple(index_at)].set(smallest)
    longest = shape.index(max(shape))
    index_at[longest] = (index_at[longest] + 1) % shape[longest]
    return values.at[tuple(index_at)].set(top_value)


def block_scale(stream_key, shape, cuts, least, largest):
    level = 1.0
    for axis_at, blocks in cuts:
        draws = jax.random.uniform(jax.random.fold_in(jax.random.fold_in(stream_key, 6), axis_at), (blocks,), jnp.float32, least / len(cuts), largest / len(cuts))
        level = level * jnp.repeat(jnp.exp(draws), shape[axis_at] // blocks).reshape((-1,) + (1,) * (len(shape) - 1 - axis_at))
    return level


def bell_draw(key, dims, scale, bound, cuts=(), kind=jnp.bfloat16):
    loudness = block_scale(key, dims, cuts, -0.22, 0.18) if cuts else 1.0
    values = jax.random.normal(key, dims, jnp.float32) * scale * loudness
    return jnp.minimum(jnp.maximum(values, -bound), bound).astype(kind)


def setup_inputs(seed: int = 0) -> dict:
    key_of = jax.random.split(jax.random.key(seed), 13)
    return {
        "features": bell_draw(key_of[0], (ATOMS, C), 1.0, 6.0, ((0, 256),)),
        "positions": draw_positions(jax.random.fold_in(key_of[12], 71), 0),
        "atom_count": draw_atom_count(jax.random.fold_in(key_of[12], 71), 0),
        "kgrid": set_ends(jax.random.randint(key_of[3], (3, K), -6, 7), jax.random.fold_in(key_of[3], 1), -6, 6).astype(jnp.int32),
        "k_filter": jnp.clip(jnp.exp(jax.random.uniform(key_of[4], (K, C), jnp.float32, math.log(0.1), math.log(1.0))), 0.1, 1.0),
        "w_mix": bell_draw(key_of[5], (C, C), C ** -0.5, 0.5, (), jnp.float32),
        "w_recv": bell_draw(key_of[6], (C, C), C ** -0.5, 0.5),
        "w_send": bell_draw(key_of[7], (C, C), C ** -0.5, 0.5),
        "w_basis": bell_draw(key_of[8], (NB, C), NB ** -0.5, 2.0),
        "w_out": bell_draw(key_of[9], (C, C), C ** -0.5, 0.5),
        "edge_basis": jnp.clip(jax.random.uniform(key_of[10], (NB, EDGES), jnp.float32, -1.0, 1.0) * block_scale(key_of[10], (NB, EDGES), ((1, 256),), -0.4, 0.0), -1.0, 1.0).astype(jnp.bfloat16),
        "senders": draw_senders(jax.random.fold_in(key_of[12], 71), 0),
    }


def phase_tables(k_rows, coords):
    wave = k_rows.astype(jnp.float32)
    phase = (wave[0][:, None] * coords[0][None, :] + wave[1][:, None] * coords[1][None, :] + wave[2][:, None] * coords[2][None, :]) * (2.0 * math.pi)
    return (jnp.cos(phase).astype(jnp.bfloat16), jnp.sin(phase).astype(jnp.bfloat16))

def factor_block(k_rows, coords, masked):
    cosines, sines = phase_tables(k_rows, coords)
    return jnp.concatenate([jnp.dot(cosines, masked, preferred_element_type=jnp.float32), jnp.dot(sines, masked, preferred_element_type=jnp.float32)], axis=1)

def k_blocks(k_rows):
    k_count = k_rows.shape[1]
    k_step = 512 if k_count % 512 == 0 else k_count
    return (k_rows.reshape(3, k_count // k_step, k_step).transpose(1, 0, 2), k_step)

def factor_rows(k_rows, coords, masked):
    blocks, k_step = k_blocks(k_rows)
    parts = lax.map(lambda wave: factor_block(wave, coords, masked), blocks)
    return parts.reshape(k_rows.shape[1], parts.shape[2])

def project_block(k_rows, coords, filtered):
    cosines, sines = phase_tables(k_rows, coords)
    channels = filtered.shape[1] // 2
    contract = (((0,), (0,)), ((), ()))
    first_term = lax.dot_general(cosines, filtered[:, :channels], contract, preferred_element_type=jnp.float32)
    second_term = lax.dot_general(sines, filtered[:, channels:], contract, preferred_element_type=jnp.float32)
    return first_term + second_term

def project_rows(running, k_rows, coords, filtered):
    blocks, k_step = k_blocks(k_rows)
    pieces = filtered.reshape(blocks.shape[0], k_step, filtered.shape[1])

    def add_block(summed, operands):
        return (summed + project_block(operands[0], coords, operands[1]), None)
    result, unused = lax.scan(add_block, running, (blocks, pieces))
    return result

def filter_rows(factor_sums, k_filter, w_mix, norm_factor):
    channels = k_filter.shape[1]
    real_part = jnp.dot(factor_sums[:, :channels] * norm_factor * k_filter, w_mix, precision=lax.Precision.HIGHEST, preferred_element_type=jnp.float32)
    imag_part = jnp.dot(factor_sums[:, channels:] * norm_factor * k_filter, w_mix, precision=lax.Precision.HIGHEST, preferred_element_type=jnp.float32)
    return jnp.concatenate([real_part, imag_part], axis=1).astype(jnp.bfloat16)

def edge_messages(recv_proj, sender_pool, senders, edge_basis, w_basis, w_out, degree):
    atom_rows = recv_proj.shape[0]
    channels = recv_proj.shape[1]
    gathered = jnp.take(sender_pool, senders, axis=0).astype(jnp.float32).reshape(atom_rows, degree, channels)
    radial = lax.dot_general(edge_basis, w_basis, (((0,), (0,)), ((), ())), preferred_element_type=jnp.float32).reshape(atom_rows, degree, channels)
    hidden = jax.nn.silu(recv_proj[:, None, :] + gathered + radial).astype(jnp.bfloat16)
    message = jnp.dot(hidden.reshape(atom_rows * degree, channels), w_out, preferred_element_type=jnp.float32)
    return lax.optimization_barrier(jnp.sum(message.reshape(atom_rows, degree, channels), axis=1)) * (1.0 / math.sqrt(degree))

def reference(features, positions, atom_count, kgrid, k_filter, w_mix, w_recv, w_send, w_basis, w_out, edge_basis, senders):
    live_mask = (jnp.arange(A_DEV, dtype=jnp.int32)[None, :] < atom_count[:, None]).astype(jnp.float32)
    masked = (features.astype(jnp.float32) * live_mask.reshape(ATOMS)[:, None]).astype(jnp.bfloat16)
    coord_blocks = positions.reshape(3, BLOCKS, A_DEV).transpose(1, 0, 2)
    masked_blocks = masked.reshape(BLOCKS, A_DEV, C)

    def add_atoms(summed, operands):
        return (summed + factor_rows(kgrid, operands[0], operands[1]), None)
    factor_sums, unused = lax.scan(add_atoms, jnp.zeros((K, 2 * C), jnp.float32), (coord_blocks, masked_blocks))
    filtered = filter_rows(factor_sums, k_filter, w_mix, 1.0 / math.sqrt(ATOMS))
    send_proj = jnp.dot(features, w_send, preferred_element_type=jnp.float32).astype(jnp.bfloat16)
    recv_proj = jnp.dot(features, w_recv, preferred_element_type=jnp.float32)
    send_grid = send_proj.reshape(SLABS, COLS, A_DEV, C)
    sender_blocks = senders.reshape(BLOCKS, A_DEV * DEG)
    basis_blocks = edge_basis.reshape(NB, BLOCKS, A_DEV * DEG).transpose(1, 0, 2)
    recv_blocks = recv_proj.reshape(BLOCKS, A_DEV, C)

    def one_block(operands):
        block_index, sender_ids, basis_rows, recv_rows, coords, mask_rows = operands
        slab_index = block_index // COLS
        column = block_index % COLS
        near_slabs = (slab_index + jnp.arange(3, dtype=jnp.int32) - 1) % SLABS
        near_cols = (column + jnp.arange(3, dtype=jnp.int32) - 1) % COLS
        sender_pool = send_grid[near_slabs][:, near_cols].reshape(9 * A_DEV, C)
        aggregate = edge_messages(recv_rows, sender_pool, sender_ids, basis_rows, w_basis, w_out, DEG)
        long_range = project_rows(jnp.zeros((A_DEV, C), jnp.float32), kgrid, coords, filtered)
        return mask_rows[:, None] * (aggregate + long_range * (4.0 / math.sqrt(K)))
    updated = lax.map(one_block, (jnp.arange(BLOCKS, dtype=jnp.int32), sender_blocks, basis_blocks, recv_blocks, coord_blocks, live_mask))
    return updated.reshape(ATOMS, C)
```

```python
import functools
import math

import jax
import jax.numpy as jnp
import numpy as np
from jax import lax
from jax.experimental import pallas as pl
from jax.experimental.pallas import tpu as pltpu
from jax.sharding import PartitionSpec as P

TOP = 6
SIDE = 2 * TOP + 1
XY_ROWS = 88
WAVE_ROWS = 2304
DEVICES = 256
ROWS_EACH = WAVE_ROWS // DEVICES
PARTS = 4
COS_TERMS = (
    0.999999989059022, -19.7392044994538, 64.93911745989, -85.4501395308031,
    60.1676309503793, -25.9675992464965, 6.52865815867317,
)
VMEM_LIMIT = 48 * 2**20


def wave_layout():
    flat = [(0, 0)] + [(kx, 0) for kx in range(1, TOP + 1)]
    flat += [(kx, ky) for ky in range(1, TOP + 1) for kx in range(-TOP, TOP + 1)]
    codes = np.full((WAVE_ROWS,), -1, np.int32)
    xy = np.zeros((2, XY_ROWS), np.float32)

    def code(kx, ky, kz):
        return ((kz + TOP) * SIDE + ky + TOP) * SIDE + kx + TOP

    for row, (kx, ky) in enumerate(flat):
        xy[0, row], xy[1, row] = kx, ky
        for kz in range(1, TOP + 1):
            base = (kz - 1) * 4 * XY_ROWS + row
            codes[base] = code(kx, ky, kz)
            codes[base + 2 * XY_ROWS] = code(kx, ky, kz)
            if row > 0:
                codes[base + XY_ROWS] = code(-kx, -ky, kz)
                codes[base + 3 * XY_ROWS] = code(-kx, -ky, kz)
        base = TOP * 4 * XY_ROWS + row
        codes[base] = code(kx, ky, 0)
        if row > 0:
            codes[base + XY_ROWS] = code(kx, ky, 0)
    return xy, codes.reshape(ROWS_EACH, DEVICES)


XY, CODES = wave_layout()


def turn_waves(turns):
    rest = turns - jnp.floor(turns + 0.5)
    quarter = rest - 0.25
    quarter = jnp.where(quarter < -0.5, quarter + 1.0, quarter)

    def cosine(part):
        square = part * part
        total = jnp.full_like(square, COS_TERMS[-1])
        for term in COS_TERMS[-2::-1]:
            total = total * square + term
        return total

    return cosine(rest), cosine(quarter)


def table_tile(xy_ref, pos_ref, first, width):
    wide = (XY_ROWS, width)
    coords = [jnp.broadcast_to(pos_ref[d : d + 1, first : first + width], wide) for d in range(2)]
    flat_turns = (
        jnp.broadcast_to(xy_ref[0][:, :1], wide) * coords[0]
        + jnp.broadcast_to(xy_ref[1][:, :1], wide) * coords[1]
    )
    cos_xy, sin_xy = turn_waves(flat_turns)
    steps = lax.broadcasted_iota(jnp.int32, (8, width), 0).astype(jnp.float32)
    cos_z, sin_z = turn_waves(
        steps * jnp.broadcast_to(pos_ref[2:3, first : first + width], (8, width))
    )
    rows = []
    for kz in range(1, TOP + 1):
        cos_k = jnp.broadcast_to(cos_z[kz : kz + 1], wide)
        sin_k = jnp.broadcast_to(sin_z[kz : kz + 1], wide)
        both_cos, both_sin = cos_xy * cos_k, sin_xy * sin_k
        sin_cos, cos_sin = sin_xy * cos_k, cos_xy * sin_k
        rows += [both_cos - both_sin, both_cos + both_sin, cos_sin + sin_cos, cos_sin - sin_cos]
    rows += [cos_xy, sin_xy, jnp.zeros((WAVE_ROWS - 26 * XY_ROWS, width), jnp.float32)]
    return jnp.concatenate(rows, axis=0).astype(jnp.bfloat16)


def factor_kernel(count_ref, xy_ref, pos_ref, features_ref, sums_ref, table_ref):
    atoms, channels = features_ref.shape
    features = features_ref[...]
    live = lax.broadcasted_iota(jnp.int32, (atoms, channels), 0) < count_ref[0]
    masked = jnp.where(live, features.astype(jnp.float32), 0.0).astype(jnp.bfloat16)
    for first in range(0, atoms, 128):
        table_ref[:, first : first + 128] = table_tile(xy_ref, pos_ref, first, 128)
    for r in range(ROWS_EACH):
        sums_ref[:, r * channels : (r + 1) * channels] = jnp.dot(
            table_ref[r * DEVICES : (r + 1) * DEVICES, :],
            masked,
            preferred_element_type=jnp.float32,
        )


def factor_call(atom_count, positions, features):
    atoms, channels = features.shape
    vmem = pl.BlockSpec(memory_space=pltpu.VMEM)
    return pl.pallas_call(
        factor_kernel,
        in_specs=[pl.BlockSpec(memory_space=pltpu.SMEM), vmem, vmem, vmem],
        out_specs=vmem,
        out_shape=jax.ShapeDtypeStruct((DEVICES, ROWS_EACH * channels), jnp.float32),
        scratch_shapes=[pltpu.VMEM((WAVE_ROWS, atoms), jnp.bfloat16)],
        compiler_params=pltpu.CompilerParams(vmem_limit_bytes=VMEM_LIMIT),
        name="factor_sums",
    )(atom_count, jnp.asarray(np.broadcast_to(XY[:, :, None], (2, XY_ROWS, 128))), positions, features)


def filter_kernel(norm_factor, sums_ref, weight_ref, mix_ref, out_ref):
    channels = mix_ref.shape[0]
    total = jnp.sum(sums_ref[...], axis=0, keepdims=True)
    rows = [total[:, r * channels : (r + 1) * channels] for r in range(ROWS_EACH)]
    rows.append(jnp.zeros((16 - ROWS_EACH, channels), jnp.float32))
    scaled = jnp.concatenate(rows, axis=0) * norm_factor * weight_ref[...]
    mixed = jnp.dot(
        scaled, mix_ref[...], precision=lax.Precision.HIGHEST, preferred_element_type=jnp.float32
    )
    for r in range(ROWS_EACH):
        out_ref[:, r * channels : (r + 1) * channels] = jnp.broadcast_to(
            mixed[r : r + 1], (out_ref.shape[0], channels)
        ).astype(jnp.bfloat16)


def filter_call(sums, weights, w_mix, norm_factor):
    return pl.pallas_call(
        functools.partial(filter_kernel, norm_factor),
        out_shape=jax.ShapeDtypeStruct(sums.shape, jnp.bfloat16),
        name="filter_rows",
    )(sums, weights, w_mix)


def wave_weights(kgrid, k_filter, first):
    kx, ky, kz = kgrid[0], kgrid[1], kgrid[2]
    low = (kz < 0) | ((kz == 0) & ((ky < 0) | ((ky == 0) & (kx < 0))))
    sign = jnp.where(low, -1, 1)
    code = ((kz * sign + TOP) * SIDE + ky * sign + TOP) * SIDE + kx * sign + TOP
    mine = lax.dynamic_slice_in_dim(jnp.asarray(CODES), first, 1, 1)
    mine = jnp.pad(mine, ((0, 16 - ROWS_EACH), (0, 0)), constant_values=-1)
    same = (mine == code[None, :]).astype(jnp.float32)
    return jnp.dot(same, k_filter, precision=lax.Precision.HIGHEST)


def edge_kernel(
    degree, unroll, ids_ref, basis_ref, features_ref, recv_ref, wb_ref, wo_ref, *refs
):
    blocks, (after_ref, out_ref, pool_ref, radial_ref, part_ref, own_ref) = refs[:9], refs[9:]
    atoms, channels = features_ref.shape
    del after_ref

    @pl.when(pl.program_id(0) == 0)
    def _():
        for at, block in enumerate(blocks):
            rows = block.shape[0]
            pool_ref[at * rows : (at + 1) * rows, :] = block[...].astype(jnp.float32)

    own_ref[...] = jnp.dot(
        features_ref[...], recv_ref[...], preferred_element_type=jnp.float32
    )
    radial_ref[...] = lax.dot_general(
        basis_ref[...], wb_ref[...], (((0,), (0,)), ((), ())), preferred_element_type=jnp.float32
    )
    sublane = lax.broadcasted_iota(jnp.int32, (8, channels), 0)

    def one_atom(atom):
        own = jnp.broadcast_to(own_ref[pl.ds(atom, 1), :], (8, channels))
        total = None
        for at in range(0, degree, 8):
            edge = atom * degree + at
            rows = [
                jnp.broadcast_to(pool_ref[pl.ds(ids_ref[edge + r], 1), :], (8, channels))
                for r in range(8)
            ]
            sent = rows[0]
            for r in range(1, 8):
                sent = jnp.where(sublane == r, rows[r], sent)
            half = (sent + radial_ref[pl.ds(pl.multiple_of(edge, 8), 8), :] + own) * 0.5
            hidden = (half + half * jnp.tanh(half)).astype(jnp.bfloat16).astype(jnp.float32)
            total = hidden if total is None else total + hidden
        part_ref[pl.ds(pl.multiple_of(atom * 8, 8), 8), :] = total

    def some_atoms(step, carry):
        for u in range(unroll):
            one_atom(step * unroll + u)
        return carry

    lax.fori_loop(0, atoms // unroll, some_atoms, 0)
    summed = part_ref[pl.ds(0, atoms, stride=8), :]
    for r in range(1, 8):
        summed = summed + part_ref[pl.ds(r, atoms, stride=8), :]
    high = summed.astype(jnp.bfloat16)
    low = (summed - high.astype(jnp.float32)).astype(jnp.bfloat16)
    message = jnp.dot(high, wo_ref[...], preferred_element_type=jnp.float32) + jnp.dot(
        low, wo_ref[...], preferred_element_type=jnp.float32
    )
    out_ref[...] = message * (1.0 / math.sqrt(degree))


def edge_call(part, after, senders, edge_basis, features, w_recv, w_basis, w_out, blocks):
    atoms, channels = features.shape
    degree = senders.shape[0] // atoms
    step = 128
    steps = atoms // PARTS // step
    first = part * steps
    whole = lambda array: pl.BlockSpec(array.shape, lambda i: (0, 0), pipeline_mode=pl.Buffered(1))
    rows = sum(block.shape[0] for block in blocks)
    return pl.pallas_call(
        functools.partial(edge_kernel, degree, 8),
        grid=(steps,),
        in_specs=[
            pl.BlockSpec((step * degree,), lambda i: (first + i,), memory_space=pltpu.SMEM),
            pl.BlockSpec((edge_basis.shape[0], step * degree), lambda i: (0, first + i)),
            pl.BlockSpec((step, channels), lambda i: (first + i, 0)),
            whole(w_recv),
            whole(w_basis),
            whole(w_out),
        ]
        + [whole(block) for block in blocks]
        + [pl.BlockSpec(memory_space=pl.ANY)],
        out_specs=pl.BlockSpec((step, channels), lambda i: (i, 0)),
        out_shape=jax.ShapeDtypeStruct((atoms // PARTS, channels), jnp.float32),
        scratch_shapes=[
            pltpu.VMEM((rows, channels), jnp.float32),
            pltpu.VMEM((step * degree, channels), jnp.float32),
            pltpu.VMEM((step * 8, channels), jnp.float32),
            pltpu.VMEM((step, channels), jnp.float32),
        ],
        compiler_params=pltpu.CompilerParams(vmem_limit_bytes=VMEM_LIMIT),
        cost_estimate=pl.CostEstimate(
            flops=8 * 10**9, bytes_accessed=4 * 10**6, transcendentals=10**6
        ),
        name="edge_part_%d" % part,
    )(senders, edge_basis, features, w_recv, w_basis, w_out, *blocks, after)


def final_kernel(scale, count_ref, xy_ref, pos_ref, factors_ref, *refs):
    parts, out_ref = refs[:-1], refs[-1]
    channels = out_ref.shape[1]
    factors = jnp.concatenate(
        [factors_ref[:, r * channels : (r + 1) * channels] for r in range(ROWS_EACH)], axis=0
    )
    for at, part in enumerate(parts):
        atoms = part.shape[0]
        first = at * atoms
        table = table_tile(xy_ref, pos_ref, first, atoms)
        field = lax.dot_general(
            factors, table, (((0,), (0,)), ((), ())), preferred_element_type=jnp.float32
        )
        live = first + lax.broadcasted_iota(jnp.int32, (atoms, channels), 0) < count_ref[0]
        out_ref[first : first + atoms, :] = jnp.where(live, part[...] + field.T * scale, 0.0)


def final_call(atom_count, positions, factors, parts, scale):
    atoms = sum(part.shape[0] for part in parts)
    channels = parts[0].shape[1]
    vmem = pl.BlockSpec(memory_space=pltpu.VMEM)
    return pl.pallas_call(
        functools.partial(final_kernel, scale),
        in_specs=[pl.BlockSpec(memory_space=pltpu.SMEM)] + [vmem] * (3 + len(parts)),
        out_specs=vmem,
        out_shape=jax.ShapeDtypeStruct((atoms, channels), jnp.float32),
        compiler_params=pltpu.CompilerParams(vmem_limit_bytes=VMEM_LIMIT),
        name="updated_rows",
    )(
        atom_count,
        jnp.asarray(np.broadcast_to(XY[:, :, None], (2, XY_ROWS, 128))),
        positions,
        factors,
        *parts,
    )


def shifted(array, axis, step):
    count = lax.axis_size(axis)
    return lax.ppermute(array, axis, [(i, (i + step) % count) for i in range(count)])


def per_device(
    features, positions, atom_count, kgrid, k_filter, w_mix, w_recv, w_send, w_basis, w_out,
    edge_basis, senders,
):
    atoms, channels = features.shape
    total_k = kgrid.shape[1]
    subs, slabs = lax.axis_size("sub"), lax.axis_size("slab")
    send_proj = jnp.dot(features, w_send, preferred_element_type=jnp.float32).astype(jnp.bfloat16)
    column = [shifted(send_proj, "slab", 1), send_proj, shifted(send_proj, "slab", -1)]
    before = [shifted(block, "sub", 1) for block in column]
    behind = [shifted(block, "sub", -1) for block in column]
    blocks = [block for a in range(3) for block in (before[a], column[a], behind[a])]

    sums = factor_call(atom_count, positions, features)
    sums = lax.all_to_all(sums, "sub", 0, 0, tiled=True)
    sums = jnp.sum(sums.reshape(subs, slabs, -1), axis=0)
    stage_one = sums
    sums = lax.all_to_all(sums, "slab", 0, 0, tiled=True)
    first = lax.axis_index("sub") * slabs + lax.axis_index("slab")
    weights = wave_weights(kgrid, k_filter, first)
    filtered = filter_call(sums, weights, w_mix, 1.0 / math.sqrt(atoms * DEVICES))
    spread = lax.all_to_all(filtered, "slab", 0, 0, tiled=True)
    factors = jnp.broadcast_to(spread[None], (subs,) + spread.shape).reshape(DEVICES, -1)
    factors = lax.all_to_all(factors, "sub", 0, 0, tiled=True)

    after = [stage_one, stage_one, filtered, spread]
    parts = [
        edge_call(p, after[p], senders, edge_basis, features, w_recv, w_basis, w_out, blocks)
        for p in range(PARTS)
    ]
    return final_call(atom_count, positions, factors, parts, 4.0 / math.sqrt(total_k))


def solution(mesh):
    placed = (
        P(("slab", "sub"), None),
        P(None, ("slab", "sub")),
        P(("slab", "sub")),
        P(), P(), P(), P(), P(), P(), P(),
        P(None, ("slab", "sub")),
        P(("slab", "sub")),
    )
    return jax.shard_map(
        per_device, mesh=mesh, in_specs=placed, out_specs=P(("slab", "sub"), None), check_vma=False
    )
```

```python
import functools
import math

import jax
import jax.numpy as jnp
import numpy as np
from jax import lax
from jax.experimental import pallas as pl
from jax.experimental.pallas import tpu as pltpu
from jax.sharding import PartitionSpec as P

TOP = 6
SIDE = 2 * TOP + 1
XY_ROWS = 88
WAVE_ROWS = 2304
DEVICES = 256
ROWS_EACH = WAVE_ROWS // DEVICES
PARTS = (320, 320, 384)
UNROLL = 16
BUFFERS = 4
COS_TERMS = (
    0.999999989059022, -19.7392044994538, 64.93911745989, -85.4501395308031,
    60.1676309503793, -25.9675992464965, 6.52865815867317,
)
VMEM_LIMIT = 60 * 2**20


def wave_layout():
    flat = [(0, 0)] + [(kx, 0) for kx in range(1, TOP + 1)]
    flat += [(kx, ky) for ky in range(1, TOP + 1) for kx in range(-TOP, TOP + 1)]
    codes = np.full((WAVE_ROWS,), -1, np.int32)
    xy = np.zeros((XY_ROWS, 2), np.float32)

    def code(kx, ky, kz):
        return ((kz + TOP) * SIDE + ky + TOP) * SIDE + kx + TOP

    for row, (kx, ky) in enumerate(flat):
        xy[row] = kx, ky
        for kz in range(1, TOP + 1):
            base = (kz - 1) * 4 * XY_ROWS + row
            codes[base] = code(kx, ky, kz)
            codes[base + 2 * XY_ROWS] = code(kx, ky, kz)
            if row > 0:
                codes[base + XY_ROWS] = code(-kx, -ky, kz)
                codes[base + 3 * XY_ROWS] = code(-kx, -ky, kz)
        base = TOP * 4 * XY_ROWS + row
        codes[base] = code(kx, ky, 0)
        if row > 0:
            codes[base + XY_ROWS] = code(kx, ky, 0)
    return xy, codes.reshape(ROWS_EACH, DEVICES)


XY, CODES = wave_layout()


def turn_waves(turns):
    rest = turns - jnp.floor(turns + 0.5)
    quarter = rest - 0.25
    quarter = jnp.where(quarter < -0.5, quarter + 1.0, quarter)

    def cosine(part):
        square = part * part
        total = jnp.full_like(square, COS_TERMS[-1])
        for term in COS_TERMS[-2::-1]:
            total = total * square + term
        return total

    return cosine(rest), cosine(quarter)


def table_tile(xy_ref, pos_ref, first, width):
    wide = (XY_ROWS, width)
    coords = [jnp.broadcast_to(pos_ref[d : d + 1, first : first + width], wide) for d in range(2)]
    flat_turns = (
        jnp.broadcast_to(xy_ref[:, 0:1], wide) * coords[0]
        + jnp.broadcast_to(xy_ref[:, 1:2], wide) * coords[1]
    )
    cos_xy, sin_xy = turn_waves(flat_turns)
    steps = lax.broadcasted_iota(jnp.int32, (8, width), 0).astype(jnp.float32)
    cos_z, sin_z = turn_waves(
        steps * jnp.broadcast_to(pos_ref[2:3, first : first + width], (8, width))
    )
    rows = []
    for kz in range(1, TOP + 1):
        cos_k = jnp.broadcast_to(cos_z[kz : kz + 1], wide)
        sin_k = jnp.broadcast_to(sin_z[kz : kz + 1], wide)
        both_cos, both_sin = cos_xy * cos_k, sin_xy * sin_k
        sin_cos, cos_sin = sin_xy * cos_k, cos_xy * sin_k
        rows += [both_cos - both_sin, both_cos + both_sin, cos_sin + sin_cos, cos_sin - sin_cos]
    rows += [cos_xy, sin_xy, jnp.zeros((WAVE_ROWS - 26 * XY_ROWS, width), jnp.float32)]
    return jnp.concatenate(rows, axis=0).astype(jnp.bfloat16)


def factor_kernel(count_ref, xy_ref, pos_ref, features_ref, sums_ref, table_ref):
    atoms, channels = features_ref.shape
    features = features_ref[...]
    live = lax.broadcasted_iota(jnp.int32, (atoms, channels), 0) < count_ref[0]
    masked = jnp.where(live, features.astype(jnp.float32), 0.0).astype(jnp.bfloat16)
    for first in range(0, atoms, 128):
        table_ref[:, first : first + 128] = table_tile(xy_ref, pos_ref, first, 128)
    for r in range(ROWS_EACH):
        sums_ref[:, r * channels : (r + 1) * channels] = jnp.dot(
            table_ref[r * DEVICES : (r + 1) * DEVICES, :],
            masked,
            preferred_element_type=jnp.float32,
        )


def factor_call(atom_count, positions, features):
    atoms, channels = features.shape
    vmem = pl.BlockSpec(memory_space=pltpu.VMEM)
    return pl.pallas_call(
        factor_kernel,
        in_specs=[pl.BlockSpec(memory_space=pltpu.SMEM), vmem, vmem, vmem],
        out_specs=vmem,
        out_shape=jax.ShapeDtypeStruct((DEVICES, ROWS_EACH * channels), jnp.float32),
        scratch_shapes=[pltpu.VMEM((WAVE_ROWS, atoms), jnp.bfloat16)],
        compiler_params=pltpu.CompilerParams(vmem_limit_bytes=VMEM_LIMIT),
        name="factor_sums",
    )(atom_count, jnp.asarray(XY), positions, features)


def stage_kernel(sums_ref, out_ref):
    total = sums_ref[0]
    for at in range(1, sums_ref.shape[0]):
        total = total + sums_ref[at]
    for at in range(out_ref.shape[0]):
        out_ref[at] = total[at : at + 1]


def stage_call(sums):
    return pl.pallas_call(
        stage_kernel,
        out_shape=jax.ShapeDtypeStruct((sums.shape[1], 1, sums.shape[2]), jnp.float32),
        name="stage_sums",
    )(sums)


def filter_kernel(norm_factor, sums_ref, weight_ref, mix_ref, out_ref):
    channels = mix_ref.shape[0]
    count = sums_ref.shape[0]
    total = sums_ref[0]
    for at in range(1, count):
        total = total + sums_ref[at]
    rows = [total[:, r * channels : (r + 1) * channels] for r in range(ROWS_EACH)]
    rows.append(jnp.zeros((16 - ROWS_EACH, channels), jnp.float32))
    scaled = jnp.concatenate(rows, axis=0) * norm_factor * weight_ref[...]
    mixed = jnp.dot(
        scaled, mix_ref[...], precision=lax.Precision.HIGHEST, preferred_element_type=jnp.float32
    )
    line = jnp.concatenate([mixed[r : r + 1] for r in range(ROWS_EACH)], axis=1)
    for at in range(count):
        out_ref[at] = line


def filter_call(sums, weights, w_mix, norm_factor):
    return pl.pallas_call(
        functools.partial(filter_kernel, norm_factor),
        out_shape=jax.ShapeDtypeStruct(sums.shape, jnp.float32),
        name="filter_rows",
    )(sums, weights, w_mix)


def spread_kernel(rows_ref, out_ref, line_ref):
    for at in range(rows_ref.shape[0]):
        line_ref[at : at + 1, :] = rows_ref[at]
    lines = line_ref[...].astype(jnp.bfloat16)
    for at in range(out_ref.shape[0]):
        out_ref[at] = lines


def spread_call(rows, copies):
    count, _, width = rows.shape
    return pl.pallas_call(
        spread_kernel,
        out_shape=jax.ShapeDtypeStruct((copies, count, width), jnp.bfloat16),
        scratch_shapes=[pltpu.VMEM((count, width), jnp.float32)],
        name="spread_rows",
    )(rows)


def wave_weights(kgrid, k_filter, first):
    kx, ky, kz = kgrid[0], kgrid[1], kgrid[2]
    low = (kz < 0) | ((kz == 0) & ((ky < 0) | ((ky == 0) & (kx < 0))))
    sign = jnp.where(low, -1, 1)
    code = ((kz * sign + TOP) * SIDE + ky * sign + TOP) * SIDE + kx * sign + TOP
    mine = lax.dynamic_slice_in_dim(jnp.asarray(CODES), first, 1, 1)
    mine = jnp.pad(mine, ((0, 16 - ROWS_EACH), (0, 0)), constant_values=-1)
    same = (mine == code[None, :]).astype(jnp.float32)
    return jnp.dot(same, k_filter, precision=lax.Precision.HIGHEST)


def edge_kernel(
    degree, first, ids_ref, basis_ref, features_ref, recv_ref, wb_ref, wo_ref, *refs
):
    blocks, refs = refs[:9], refs[9:]
    (after_ref, out_ref, pool_ref, radial_ref, part_ref, own_ref, wide_ref), refs = refs[:7], refs[7:]
    buffers, arrivals = refs[:BUFFERS], refs[BUFFERS:]
    atoms, channels = out_ref.shape
    del after_ref
    edges = UNROLL * degree
    lines = edges // 128
    chunks = atoms // UNROLL

    def fetch(chunk, at):
        source = ids_ref.at[pl.ds(first * degree // 128 + chunk * lines, lines), :]
        return pltpu.make_async_copy(source, buffers[at], arrivals[at])

    for at in range(BUFFERS):
        fetch(at, at).start()

    slab_even = lax.rem(lax.axis_index("slab"), 2) == 0
    sub_even = lax.rem(lax.axis_index("sub"), 2) == 0
    slab_place = (1, jnp.where(slab_even, 2, 0), jnp.where(slab_even, 0, 2))
    sub_place = (1, jnp.where(sub_even, 2, 0), jnp.where(sub_even, 0, 2))
    for at, block in enumerate(blocks):
        rows = block.shape[0]
        place = pl.multiple_of((slab_place[at // 3] * 3 + sub_place[at % 3]) * rows, rows)
        pool_ref[pl.ds(place, rows), :] = block[...].astype(jnp.float32)

    own_ref[...] = jnp.dot(
        features_ref[first : first + atoms, :], recv_ref[...], preferred_element_type=jnp.float32
    )

    basis_rows = wb_ref.shape[0]
    groups = 128 // basis_rows
    stacked = jnp.concatenate([wb_ref[...].astype(jnp.float32)] * groups, axis=0)
    group_of = lax.broadcasted_iota(jnp.int32, stacked.shape, 0) // basis_rows
    for g in range(groups):
        wide_ref[:, g * channels : (g + 1) * channels] = jnp.where(
            group_of == g, stacked, 0.0
        ).astype(jnp.bfloat16)

    span = groups * 128

    def radial_block(step, carry):
        base = pl.multiple_of(step * span, span)
        values = basis_ref[:, pl.ds(pl.multiple_of(first * degree + base, span), span)]
        values = values.astype(jnp.float32)
        stack = jnp.concatenate([values[:, g * 128 : (g + 1) * 128] for g in range(groups)], axis=0)
        turned = stack.T.astype(jnp.bfloat16)
        for g in range(0, groups, 2):
            both = jnp.dot(
                turned,
                wide_ref[:, g * channels : (g + 2) * channels],
                preferred_element_type=jnp.float32,
            )
            radial_ref[pl.ds(base + g * 128, 128), :] = both[:, :channels]
            radial_ref[pl.ds(base + (g + 1) * 128, 128), :] = both[:, channels:]
        return carry

    lax.fori_loop(0, atoms * degree // span, radial_block, 0)
    sublane = lax.broadcasted_iota(jnp.int32, (8, channels), 0)
    at_sublane = [sublane == r for r in range(8)]

    def some_atoms(chunk, ids):
        own = own_ref.at[pl.ds(pl.multiple_of(chunk * UNROLL, UNROLL), UNROLL), :]
        part = part_ref.at[pl.ds(pl.multiple_of(chunk * UNROLL * 8, UNROLL * 8), UNROLL * 8), :]
        radial = radial_ref.at[pl.ds(pl.multiple_of(chunk * edges, edges), edges), :]
        for u in range(UNROLL):
            mine = jnp.broadcast_to(own[u : u + 1, :], (8, channels))
            total = None
            for edge in range(u * degree, (u + 1) * degree, 8):
                sent = None
                for r in range(8):
                    sender = ids[(edge + r) // 128, (edge + r) % 128]
                    row = jnp.broadcast_to(pool_ref[pl.ds(sender, 1), :], (8, channels))
                    sent = row if sent is None else jnp.where(at_sublane[r], row, sent)
                half = (sent + radial[edge : edge + 8, :] + mine) * 0.5
                hidden = (half + half * jnp.tanh(half)).astype(jnp.bfloat16).astype(jnp.float32)
                total = hidden if total is None else total + hidden
            part[u * 8 : u * 8 + 8, :] = total

    def round_of_chunks(step, carry):
        for at in range(BUFFERS):
            chunk = step * BUFFERS + at
            fetch(chunk, at).wait()
            some_atoms(chunk, buffers[at])
            fetch(jnp.minimum(chunk + BUFFERS, chunks - 1), at).start()
        return carry

    lax.fori_loop(0, chunks // BUFFERS, round_of_chunks, 0)
    for at in range(BUFFERS):
        fetch(chunks - 1, at).wait()
    summed = part_ref[pl.ds(0, atoms, stride=8), :]
    for r in range(1, 8):
        summed = summed + part_ref[pl.ds(r, atoms, stride=8), :]
    high = summed.astype(jnp.bfloat16)
    low = (summed - high.astype(jnp.float32)).astype(jnp.bfloat16)
    message = jnp.dot(high, wo_ref[...], preferred_element_type=jnp.float32) + jnp.dot(
        low, wo_ref[...], preferred_element_type=jnp.float32
    )
    out_ref[...] = message * (1.0 / math.sqrt(degree))


def edge_call(part, after, senders, edge_basis, features, w_recv, w_basis, w_out, blocks):
    channels = features.shape[1]
    degree = senders.shape[0] // features.shape[0]
    atoms, first = PARTS[part], sum(PARTS[:part])
    vmem = pl.BlockSpec(memory_space=pltpu.VMEM)
    rows = sum(block.shape[0] for block in blocks)
    return pl.pallas_call(
        functools.partial(edge_kernel, degree, first),
        in_specs=[vmem] * (6 + len(blocks)) + [pl.BlockSpec(memory_space=pl.ANY)],
        out_specs=vmem,
        out_shape=jax.ShapeDtypeStruct((atoms, channels), jnp.float32),
        scratch_shapes=[
            pltpu.VMEM((rows, channels), jnp.float32),
            pltpu.VMEM((atoms * degree, channels), jnp.float32),
            pltpu.VMEM((atoms * 8, channels), jnp.float32),
            pltpu.VMEM((atoms, channels), jnp.float32),
            pltpu.VMEM((128, 128 // w_basis.shape[0] * channels), jnp.bfloat16),
        ]
        + [pltpu.SMEM((UNROLL * degree // 128, 128), jnp.int32)] * BUFFERS
        + [pltpu.SemaphoreType.DMA] * BUFFERS,
        compiler_params=pltpu.CompilerParams(vmem_limit_bytes=VMEM_LIMIT),
        cost_estimate=pl.CostEstimate(
            flops=8 * 10**9, bytes_accessed=4 * 10**6, transcendentals=10**6
        ),
        name="edge_part_%d" % part,
    )(
        senders.reshape(-1, 128), edge_basis, features, w_recv, w_basis, w_out, *blocks, after
    )


def final_kernel(scale, count_ref, xy_ref, pos_ref, factors_ref, *refs):
    parts, out_ref = refs[:-1], refs[-1]
    channels = out_ref.shape[1]
    factors = jnp.concatenate(
        [factors_ref[:, r * channels : (r + 1) * channels] for r in range(ROWS_EACH)], axis=0
    )
    total, first = out_ref.shape[0], 0
    for part in parts:
        out_ref[first : first + part.shape[0], :] = part[...]
        first += part.shape[0]
    atoms = 256
    for first in range(0, total, atoms):
        table = table_tile(xy_ref, pos_ref, first, atoms)
        field = lax.dot_general(
            factors, table, (((0,), (0,)), ((), ())), preferred_element_type=jnp.float32
        )
        live = first + lax.broadcasted_iota(jnp.int32, (atoms, channels), 0) < count_ref[0]
        near = out_ref[first : first + atoms, :]
        out_ref[first : first + atoms, :] = jnp.where(live, near + field.T * scale, 0.0)


def final_call(atom_count, positions, factors, parts, scale):
    atoms = sum(part.shape[0] for part in parts)
    channels = parts[0].shape[1]
    vmem = pl.BlockSpec(memory_space=pltpu.VMEM)
    return pl.pallas_call(
        functools.partial(final_kernel, scale),
        in_specs=[pl.BlockSpec(memory_space=pltpu.SMEM)] + [vmem] * (3 + len(parts)),
        out_specs=vmem,
        out_shape=jax.ShapeDtypeStruct((atoms, channels), jnp.float32),
        compiler_params=pltpu.CompilerParams(vmem_limit_bytes=VMEM_LIMIT),
        name="updated_rows",
    )(
        atom_count,
        jnp.asarray(XY),
        positions,
        factors,
        *parts,
    )


def moved(array, target):
    slabs, subs = lax.axis_size("slab"), lax.axis_size("sub")
    pairs = []
    for s in range(slabs):
        for b in range(subs):
            to_s, to_b = target(s, b)
            pairs.append((s * subs + b, to_s % slabs * subs + to_b % subs))
    return lax.ppermute(array, ("slab", "sub"), pairs)


def to_core(s, b):
    return s ^ 1, b


def to_outer(s, b):
    return s + (1 if s % 2 else -1), b


def to_column(s, b):
    return s, b ^ 1


def to_beyond(s, b):
    return s, b + (-2 if b % 2 else 2)


def per_device(
    features, positions, atom_count, kgrid, k_filter, w_mix, w_recv, w_send, w_basis, w_out,
    edge_basis, senders,
):
    atoms, channels = features.shape
    total_k = kgrid.shape[1]
    subs, slabs = lax.axis_size("sub"), lax.axis_size("slab")
    send_proj = jnp.dot(features, w_send, preferred_element_type=jnp.float32).astype(jnp.bfloat16)
    outer = moved(send_proj, to_outer)
    near = moved(send_proj, to_column)
    core = moved(send_proj, to_core)
    outer_near = moved(outer, to_column)
    beyond = moved(near, to_beyond)
    core_near = moved(near, to_core)
    outer_beyond = moved(outer_near, to_beyond)
    core_beyond = moved(beyond, to_core)
    blocks = [
        send_proj, near, beyond, core, core_near, core_beyond, outer, outer_near, outer_beyond
    ]

    sums = factor_call(atom_count, positions, features)
    sums = lax.all_to_all(sums, "sub", 0, 0, tiled=True)
    stage_one = stage_call(sums.reshape(subs, slabs, -1))
    sums = lax.all_to_all(stage_one, "slab", 0, 0, tiled=True)
    first = lax.axis_index("sub") * slabs + lax.axis_index("slab")
    weights = wave_weights(kgrid, k_filter, first)
    filtered = filter_call(sums, weights, w_mix, 1.0 / math.sqrt(atoms * DEVICES))
    rows = lax.all_to_all(filtered, "slab", 0, 0, tiled=True)
    spread = spread_call(rows, subs)
    factors = lax.all_to_all(spread.reshape(DEVICES, -1), "sub", 0, 0, tiled=True)

    after = [stage_one, filtered, spread]
    parts = [
        edge_call(p, after[p], senders, edge_basis, features, w_recv, w_basis, w_out, blocks)
        for p in range(len(PARTS))
    ]
    return final_call(atom_count, positions, factors, parts, 4.0 / math.sqrt(total_k))


def solution(mesh):
    placed = (
        P(("slab", "sub"), None),
        P(None, ("slab", "sub")),
        P(("slab", "sub")),
        P(), P(), P(), P(), P(), P(), P(),
        P(None, ("slab", "sub")),
        P(("slab", "sub")),
    )
    return jax.shard_map(
        per_device, mesh=mesh, in_specs=placed, out_specs=P(("slab", "sub"), None), check_vma=False
    )
```

```python
import functools
import math

import jax
import jax.numpy as jnp
import numpy as np
from jax import lax
from jax.experimental import pallas as pl
from jax.experimental.pallas import tpu as pltpu
from jax.sharding import PartitionSpec as P

TOP = 6
SIDE = 2 * TOP + 1
XY_ROWS = 88
WAVE_ROWS = 2304
DEVICES = 256
ROWS_EACH = WAVE_ROWS // DEVICES
PARTS = (256, 256, 512)
PLANE = 4
UNROLL = 16
BUFFERS = 4
COS_TERMS = (
    0.999999989059022, -19.7392044994538, 64.93911745989, -85.4501395308031,
    60.1676309503793, -25.9675992464965, 6.52865815867317,
)
SMALL_VMEM, TABLE_VMEM, LARGE_VMEM = 6 * 2**20, 14 * 2**20, 60 * 2**20


def wave_layout():
    flat = [(0, 0)] + [(kx, 0) for kx in range(1, TOP + 1)]
    flat += [(kx, ky) for ky in range(1, TOP + 1) for kx in range(-TOP, TOP + 1)]
    codes = np.full((WAVE_ROWS,), -1, np.int32)
    xy = np.zeros((XY_ROWS, 2), np.float32)

    def code(kx, ky, kz):
        return ((kz + TOP) * SIDE + ky + TOP) * SIDE + kx + TOP

    for row, (kx, ky) in enumerate(flat):
        xy[row] = kx, ky
        for kz in range(1, TOP + 1):
            base = (kz - 1) * 4 * XY_ROWS + row
            codes[base] = code(kx, ky, kz)
            codes[base + 2 * XY_ROWS] = code(kx, ky, kz)
            if row > 0:
                codes[base + XY_ROWS] = code(-kx, -ky, kz)
                codes[base + 3 * XY_ROWS] = code(-kx, -ky, kz)
        base = TOP * 4 * XY_ROWS + row
        codes[base] = code(kx, ky, 0)
        if row > 0:
            codes[base + XY_ROWS] = code(kx, ky, 0)
    return xy, codes.reshape(ROWS_EACH, DEVICES)


XY, CODES = wave_layout()


def turn_waves(turns):
    rest = turns - jnp.floor(turns + 0.5)
    quarter = rest - 0.25
    quarter = jnp.where(quarter < -0.5, quarter + 1.0, quarter)

    def cosine(part):
        square = part * part
        total = jnp.full_like(square, COS_TERMS[-1])
        for term in COS_TERMS[-2::-1]:
            total = total * square + term
        return total

    return cosine(rest), cosine(quarter)


def table_tile(xy_ref, pos_ref, first, width):
    wide = (XY_ROWS, width)
    coords = [jnp.broadcast_to(pos_ref[d : d + 1, first : first + width], wide) for d in range(2)]
    flat_turns = (
        jnp.broadcast_to(xy_ref[:, 0:1], wide) * coords[0]
        + jnp.broadcast_to(xy_ref[:, 1:2], wide) * coords[1]
    )
    cos_xy, sin_xy = turn_waves(flat_turns)
    steps = lax.broadcasted_iota(jnp.int32, (8, width), 0).astype(jnp.float32)
    cos_z, sin_z = turn_waves(
        steps * jnp.broadcast_to(pos_ref[2:3, first : first + width], (8, width))
    )
    rows = []
    for kz in range(1, TOP + 1):
        cos_k = jnp.broadcast_to(cos_z[kz : kz + 1], wide)
        sin_k = jnp.broadcast_to(sin_z[kz : kz + 1], wide)
        both_cos, both_sin = cos_xy * cos_k, sin_xy * sin_k
        sin_cos, cos_sin = sin_xy * cos_k, cos_xy * sin_k
        rows += [both_cos - both_sin, both_cos + both_sin, cos_sin + sin_cos, cos_sin - sin_cos]
    rows += [cos_xy, sin_xy, jnp.zeros((WAVE_ROWS - 26 * XY_ROWS, width), jnp.float32)]
    return jnp.concatenate(rows, axis=0).astype(jnp.bfloat16)


def hbm():
    return pl.BlockSpec(memory_space=pltpu.HBM)


def vmem():
    return pl.BlockSpec(memory_space=pltpu.VMEM)


def limit(size):
    return pltpu.CompilerParams(vmem_limit_bytes=size)


def loads(sources, targets, arrivals):
    copies = [
        pltpu.make_async_copy(source, target, arrivals.at[at])
        for at, (source, target) in enumerate(zip(sources, targets))
    ]
    for copy in copies:
        copy.start()
    return copies


def factor_kernel(
    count_ref, xy_hbm, pos_hbm, features_hbm, *refs
):
    after_refs, refs = refs[:-6], refs[-6:]
    sums_ref, table_ref, xy_ref, pos_ref, features_ref, arrivals = refs
    del after_refs
    copies = loads((xy_hbm, pos_hbm, features_hbm), (xy_ref, pos_ref, features_ref), arrivals)
    atoms, channels = features_ref.shape
    copies[0].wait()
    copies[1].wait()
    for first in range(0, atoms, 128):
        table_ref[:, first : first + 128] = table_tile(xy_ref, pos_ref, first, 128)
    copies[2].wait()
    live = lax.broadcasted_iota(jnp.int32, (atoms, channels), 0) < count_ref[0]
    masked = jnp.where(live, features_ref[...].astype(jnp.float32), 0.0).astype(jnp.bfloat16)
    for r in range(ROWS_EACH):
        sums_ref[:, r * channels : (r + 1) * channels] = jnp.dot(
            table_ref[r * DEVICES : (r + 1) * DEVICES, :],
            masked,
            preferred_element_type=jnp.float32,
        )


def factor_call(atom_count, positions, features, after):
    atoms, channels = features.shape
    return pl.pallas_call(
        factor_kernel,
        in_specs=[pl.BlockSpec(memory_space=pltpu.SMEM), hbm(), hbm(), hbm()]
        + [pl.BlockSpec(memory_space=pl.ANY)] * len(after),
        out_specs=vmem(),
        out_shape=jax.ShapeDtypeStruct((DEVICES, ROWS_EACH * channels), jnp.float32),
        scratch_shapes=[
            pltpu.VMEM((WAVE_ROWS, atoms), jnp.bfloat16),
            pltpu.VMEM(XY.shape, jnp.float32),
            pltpu.VMEM(positions.shape, jnp.float32),
            pltpu.VMEM(features.shape, jnp.bfloat16),
            pltpu.SemaphoreType.DMA((3,)),
        ],
        compiler_params=limit(LARGE_VMEM),
        name="factor_sums",
    )(atom_count, jnp.asarray(XY), positions, features, *after)


def stage_kernel(sums_ref, out_ref):
    rows = out_ref.shape[1]
    total = sums_ref[0:rows, :]
    for at in range(rows, sums_ref.shape[0], rows):
        total = total + sums_ref[at : at + rows, :]
    for at in range(out_ref.shape[0]):
        out_ref[at] = total


def stage_call(sums, sources, copies):
    return pl.pallas_call(
        stage_kernel,
        out_specs=vmem(),
        out_shape=jax.ShapeDtypeStruct(
            (copies, sums.shape[0] // sources, sums.shape[1]), jnp.float32
        ),
        compiler_params=limit(SMALL_VMEM),
        name="stage_sums",
    )(sums)


def filter_kernel(norm_factor, sums_ref, weight_ref, mix_hbm, out_ref, mix_ref, arrivals):
    copies = loads((mix_hbm,), (mix_ref,), arrivals)
    channels = mix_ref.shape[0]
    total = sums_ref[0]
    for at in range(1, sums_ref.shape[0]):
        total = total + sums_ref[at]
    count = total.shape[0]
    scaled = jnp.concatenate(
        [total[:, r * channels : (r + 1) * channels] for r in range(ROWS_EACH)], axis=0
    )
    scaled = scaled * norm_factor * weight_ref[...]
    copies[0].wait()
    mixed = jnp.dot(
        scaled, mix_ref[...], precision=lax.Precision.HIGHEST, preferred_element_type=jnp.float32
    )
    lines = jnp.concatenate(
        [mixed[r * count : (r + 1) * count] for r in range(ROWS_EACH)], axis=1
    ).astype(jnp.bfloat16)
    for at in range(out_ref.shape[0]):
        out_ref[at] = lines


def filter_call(sums, weights, w_mix, norm_factor, copies):
    return pl.pallas_call(
        functools.partial(filter_kernel, norm_factor),
        in_specs=[vmem(), vmem(), hbm()],
        out_specs=vmem(),
        out_shape=jax.ShapeDtypeStruct((copies,) + sums.shape[1:], jnp.bfloat16),
        scratch_shapes=[pltpu.VMEM(w_mix.shape, jnp.float32), pltpu.SemaphoreType.DMA((1,))],
        compiler_params=limit(SMALL_VMEM),
        name="filter_rows",
    )(sums, weights, w_mix)


def wave_weights(kgrid, k_filter, first, count):
    kx, ky, kz = kgrid[0], kgrid[1], kgrid[2]
    low = (kz < 0) | ((kz == 0) & ((ky < 0) | ((ky == 0) & (kx < 0))))
    sign = jnp.where(low, -1, 1)
    code = ((kz * sign + TOP) * SIDE + ky * sign + TOP) * SIDE + kx * sign + TOP
    mine = lax.dynamic_slice_in_dim(jnp.asarray(CODES), first, count, 1).reshape(-1)
    same = (mine[:, None] == code[None, :]).astype(jnp.float32)
    return jnp.dot(same, k_filter, precision=lax.Precision.HIGHEST)


def edge_kernel(
    degree, first, ids_hbm, basis_hbm, features_hbm, recv_hbm, wb_hbm, wo_hbm, *refs
):
    blocks, refs = refs[:7], refs[7:]
    (after_ref, out_ref, pool_ref, radial_ref, part_ref, own_ref, wide_ref), refs = refs[:7], refs[7:]
    local, loaded, refs = refs[:6], refs[6], refs[7:]
    ids_ref, basis_ref, features_ref, recv_ref, wb_ref, wo_ref = local
    buffers, arrivals = refs[:BUFFERS], refs[BUFFERS:]
    atoms, channels = out_ref.shape
    del after_ref
    copies = loads(
        (
            ids_hbm.at[pl.ds(first * degree // 128, atoms * degree // 128), :],
            basis_hbm.at[:, pl.ds(first * degree, atoms * degree)],
            features_hbm.at[pl.ds(first, atoms), :],
            recv_hbm,
            wb_hbm,
            wo_hbm,
        ),
        local,
        loaded,
    )
    edges = UNROLL * degree
    lines = edges // 128
    chunks = atoms // UNROLL

    def fetch(chunk, at):
        source = ids_ref.at[pl.ds(chunk * lines, lines), :]
        return pltpu.make_async_copy(source, buffers[at], arrivals[at])

    slab_even = lax.rem(lax.axis_index("slab"), 2) == 0
    sub_even = lax.rem(lax.axis_index("sub"), 2) == 0
    slab_place = (1, jnp.where(slab_even, 2, 0), jnp.where(slab_even, 0, 2))
    sub_place = (1, jnp.where(sub_even, 2, 0), jnp.where(sub_even, 0, 2))
    rows = blocks[0].shape[0]
    at = 0
    for block in blocks:
        for first_row in range(0, block.shape[0], rows):
            place = pl.multiple_of((slab_place[at // 3] * 3 + sub_place[at % 3]) * rows, rows)
            pool_ref[pl.ds(place, rows), :] = block[first_row : first_row + rows, :].astype(
                jnp.float32
            )
            at += 1

    for copy in copies:
        copy.wait()
    for at in range(BUFFERS):
        fetch(at, at).start()
    own_ref[...] = jnp.dot(features_ref[...], recv_ref[...], preferred_element_type=jnp.float32)

    basis_rows = wb_ref.shape[0]
    groups = 128 // basis_rows
    stacked = jnp.concatenate([wb_ref[...].astype(jnp.float32)] * groups, axis=0)
    group_of = lax.broadcasted_iota(jnp.int32, stacked.shape, 0) // basis_rows
    for g in range(groups):
        wide_ref[:, g * channels : (g + 1) * channels] = jnp.where(
            group_of == g, stacked, 0.0
        ).astype(jnp.bfloat16)

    span = groups * 128

    def radial_block(step, carry):
        base = pl.multiple_of(step * span, span)
        values = basis_ref[:, pl.ds(base, span)]
        values = values.astype(jnp.float32)
        stack = jnp.concatenate([values[:, g * 128 : (g + 1) * 128] for g in range(groups)], axis=0)
        turned = stack.T.astype(jnp.bfloat16)
        for g in range(0, groups, 2):
            both = jnp.dot(
                turned,
                wide_ref[:, g * channels : (g + 2) * channels],
                preferred_element_type=jnp.float32,
            )
            radial_ref[pl.ds(base + g * 128, 128), :] = both[:, :channels]
            radial_ref[pl.ds(base + (g + 1) * 128, 128), :] = both[:, channels:]
        return carry

    lax.fori_loop(0, atoms * degree // span, radial_block, 0)
    sublane = lax.broadcasted_iota(jnp.int32, (8, channels), 0)
    at_sublane = [sublane == r for r in range(8)]

    def some_atoms(chunk, ids):
        own = own_ref.at[pl.ds(pl.multiple_of(chunk * UNROLL, UNROLL), UNROLL), :]
        part = part_ref.at[pl.ds(pl.multiple_of(chunk * UNROLL * 8, UNROLL * 8), UNROLL * 8), :]
        radial = radial_ref.at[pl.ds(pl.multiple_of(chunk * edges, edges), edges), :]
        for u in range(UNROLL):
            mine = jnp.broadcast_to(own[u : u + 1, :], (8, channels))
            total = None
            for edge in range(u * degree, (u + 1) * degree, 8):
                sent = None
                for r in range(8):
                    sender = ids[(edge + r) // 128, (edge + r) % 128]
                    row = jnp.broadcast_to(pool_ref[pl.ds(sender, 1), :], (8, channels))
                    sent = row if sent is None else jnp.where(at_sublane[r], row, sent)
                half = (sent + radial[edge : edge + 8, :] + mine) * 0.5
                hidden = (half + half * jnp.tanh(half)).astype(jnp.bfloat16).astype(jnp.float32)
                total = hidden if total is None else total + hidden
            part[u * 8 : u * 8 + 8, :] = total

    def round_of_chunks(step, carry):
        for at in range(BUFFERS):
            chunk = step * BUFFERS + at
            fetch(chunk, at).wait()
            some_atoms(chunk, buffers[at])
            fetch(jnp.minimum(chunk + BUFFERS, chunks - 1), at).start()
        return carry

    lax.fori_loop(0, chunks // BUFFERS, round_of_chunks, 0)
    for at in range(BUFFERS):
        fetch(chunks - 1, at).wait()
    summed = part_ref[pl.ds(0, atoms, stride=8), :]
    for r in range(1, 8):
        summed = summed + part_ref[pl.ds(r, atoms, stride=8), :]
    high = summed.astype(jnp.bfloat16)
    low = (summed - high.astype(jnp.float32)).astype(jnp.bfloat16)
    message = jnp.dot(high, wo_ref[...], preferred_element_type=jnp.float32) + jnp.dot(
        low, wo_ref[...], preferred_element_type=jnp.float32
    )
    out_ref[...] = message * (1.0 / math.sqrt(degree))


def edge_call(part, after, senders, edge_basis, features, w_recv, w_basis, w_out, blocks):
    channels = features.shape[1]
    degree = senders.shape[0] // features.shape[0]
    atoms, first = PARTS[part], sum(PARTS[:part])
    rows = sum(block.shape[0] for block in blocks)
    return pl.pallas_call(
        functools.partial(edge_kernel, degree, first),
        in_specs=[hbm()] * 6 + [vmem()] * len(blocks) + [pl.BlockSpec(memory_space=pl.ANY)],
        out_specs=vmem(),
        out_shape=jax.ShapeDtypeStruct((atoms, channels), jnp.float32),
        scratch_shapes=[
            pltpu.VMEM((rows, channels), jnp.float32),
            pltpu.VMEM((atoms * degree, channels), jnp.float32),
            pltpu.VMEM((atoms * 8, channels), jnp.float32),
            pltpu.VMEM((atoms, channels), jnp.float32),
            pltpu.VMEM((128, 128 // w_basis.shape[0] * channels), jnp.bfloat16),
            pltpu.VMEM((atoms * degree // 128, 128), jnp.int32),
            pltpu.VMEM((edge_basis.shape[0], atoms * degree), jnp.bfloat16),
            pltpu.VMEM((atoms, channels), jnp.bfloat16),
            pltpu.VMEM(w_recv.shape, jnp.bfloat16),
            pltpu.VMEM(w_basis.shape, jnp.bfloat16),
            pltpu.VMEM(w_out.shape, jnp.bfloat16),
            pltpu.SemaphoreType.DMA((6,)),
        ]
        + [pltpu.SMEM((UNROLL * degree // 128, 128), jnp.int32)] * BUFFERS
        + [pltpu.SemaphoreType.DMA] * BUFFERS,
        compiler_params=limit(LARGE_VMEM),
        cost_estimate=pl.CostEstimate(
            flops=8 * 10**9, bytes_accessed=4 * 10**6, transcendentals=10**6
        ),
        name="edge_part_%d" % part,
    )(
        senders.reshape(-1, 128), edge_basis, features, w_recv, w_basis, w_out, *blocks, after
    )


def final_kernel(scale, count_ref, xy_hbm, pos_hbm, factors_ref, *refs):
    parts, (out_ref, xy_ref, pos_ref, arrivals) = refs[:-4], refs[-4:]
    copies = loads((xy_hbm, pos_hbm), (xy_ref, pos_ref), arrivals)
    channels = out_ref.shape[1]
    factors = jnp.concatenate(
        [factors_ref[:, r * channels : (r + 1) * channels] for r in range(ROWS_EACH)], axis=0
    ).T
    total, first = out_ref.shape[0], 0
    for part in parts:
        out_ref[first : first + part.shape[0], :] = part[...]
        first += part.shape[0]
    for copy in copies:
        copy.wait()
    atoms = 256
    for first in range(0, total, atoms):
        table = table_tile(xy_ref, pos_ref, first, atoms)
        field = jnp.dot(factors, table, preferred_element_type=jnp.float32)
        live = first + lax.broadcasted_iota(jnp.int32, (atoms, channels), 0) < count_ref[0]
        near = out_ref[first : first + atoms, :]
        out_ref[first : first + atoms, :] = jnp.where(live, near + field.T * scale, 0.0)


def final_call(atom_count, positions, factors, parts, scale):
    atoms = sum(part.shape[0] for part in parts)
    channels = parts[0].shape[1]
    return pl.pallas_call(
        functools.partial(final_kernel, scale),
        in_specs=[pl.BlockSpec(memory_space=pltpu.SMEM), hbm(), hbm(), vmem()]
        + [vmem()] * len(parts),
        out_specs=vmem(),
        out_shape=jax.ShapeDtypeStruct((atoms, channels), jnp.float32),
        scratch_shapes=[
            pltpu.VMEM(XY.shape, jnp.float32),
            pltpu.VMEM(positions.shape, jnp.float32),
            pltpu.SemaphoreType.DMA((2,)),
        ],
        compiler_params=limit(TABLE_VMEM),
        name="updated_rows",
    )(atom_count, jnp.asarray(XY), positions, factors, *parts)


def moved(array, target):
    slabs, subs = lax.axis_size("slab"), lax.axis_size("sub")
    pairs = []
    for s in range(slabs):
        for b in range(subs):
            to_s, to_b = target(s, b)
            pairs.append((s * subs + b, to_s % slabs * subs + to_b % subs))
    return lax.ppermute(array, ("slab", "sub"), pairs)


def to_core(s, b):
    return s ^ 1, b


def to_outer(s, b):
    return s + (1 if s % 2 else -1), b


def to_column(s, b):
    return s, b ^ 1


def to_beyond(s, b):
    return s, b + (-1 if b % 2 == 0 else 1)


def plane_groups(slabs, subs):
    return [
        [(z * PLANE + q) * subs + b for b in range(subs) for q in range(PLANE)]
        for z in range(slabs // PLANE)
    ]


def line_groups(slabs, subs):
    return [
        [(z * PLANE + q) * subs + b for z in range(slabs // PLANE)]
        for b in range(subs)
        for q in range(PLANE)
    ]


def exchanged(array, groups):
    return lax.all_to_all(array, ("slab", "sub"), 0, 0, axis_index_groups=groups, tiled=True)


def per_device(
    features, positions, atom_count, kgrid, k_filter, w_mix, w_recv, w_send, w_basis, w_out,
    edge_basis, senders,
):
    atoms, channels = features.shape
    total_k = kgrid.shape[1]
    subs, slabs = lax.axis_size("sub"), lax.axis_size("slab")
    send_proj = jnp.dot(features, w_send, preferred_element_type=jnp.float32).astype(jnp.bfloat16)
    outer = moved(send_proj, to_outer)
    near = moved(send_proj, to_column)
    beyond = moved(send_proj, to_beyond)
    outer_near = moved(send_proj, lambda s, b: to_outer(*to_column(s, b)))
    outer_beyond = moved(send_proj, lambda s, b: to_outer(*to_beyond(s, b)))
    core = moved(jnp.concatenate([send_proj, near, beyond]), to_core)
    blocks = [send_proj, near, beyond, core, outer, outer_near, outer_beyond]

    plane, line = plane_groups(slabs, subs), line_groups(slabs, subs)
    mine = lax.axis_index("sub") * PLANE + lax.axis_index("slab") % PLANE
    sums = factor_call(atom_count, positions, features, ())
    stage_one = stage_call(exchanged(sums, plane), len(plane[0]), len(line[0]))
    count = stage_one.shape[1]
    weights = wave_weights(kgrid, k_filter, mine * count, count)
    norm_factor = 1.0 / math.sqrt(atoms * DEVICES)
    filtered = filter_call(
        exchanged(stage_one, line), weights, w_mix, norm_factor, len(plane[0])
    )
    factors = exchanged(filtered, plane).reshape(DEVICES, -1)

    after = [sums, stage_one, filtered]
    parts = [
        edge_call(p, after[p], senders, edge_basis, features, w_recv, w_basis, w_out, blocks)
        for p in range(len(PARTS))
    ]
    return final_call(atom_count, positions, factors, parts, 4.0 / math.sqrt(total_k))


def solution(mesh):
    placed = (
        P(("slab", "sub"), None),
        P(None, ("slab", "sub")),
        P(("slab", "sub")),
        P(), P(), P(), P(), P(), P(), P(),
        P(None, ("slab", "sub")),
        P(("slab", "sub")),
    )
    return jax.shard_map(
        per_device, mesh=mesh, in_specs=placed, out_specs=P(("slab", "sub"), None), check_vma=False
    )
```

```python
import functools
import math

import jax
import jax.numpy as jnp
import numpy as np
from jax import lax
from jax.experimental import pallas as pl
from jax.experimental.pallas import tpu as pltpu
from jax.sharding import PartitionSpec as P

TOP = 6
SIDE = 2 * TOP + 1
XY_ROWS = 88
WAVE_ROWS = 2304
DEVICES = 256
ROWS_EACH = WAVE_ROWS // DEVICES
PARTS = (512, 512)
PLANE = 4
UNROLL = 16
BUFFERS = 4
COS_TERMS = (
    0.999999989059022, -19.7392044994538, 64.93911745989, -85.4501395308031,
    60.1676309503793, -25.9675992464965, 6.52865815867317,
)
SMALL_VMEM, TABLE_VMEM, LARGE_VMEM = 6 * 2**20, 14 * 2**20, 60 * 2**20


def wave_layout():
    flat = [(0, 0)] + [(kx, 0) for kx in range(1, TOP + 1)]
    flat += [(kx, ky) for ky in range(1, TOP + 1) for kx in range(-TOP, TOP + 1)]
    codes = np.full((WAVE_ROWS,), -1, np.int32)
    xy = np.zeros((XY_ROWS, 2), np.float32)

    def code(kx, ky, kz):
        return ((kz + TOP) * SIDE + ky + TOP) * SIDE + kx + TOP

    for row, (kx, ky) in enumerate(flat):
        xy[row] = kx, ky
        for kz in range(1, TOP + 1):
            base = (kz - 1) * 4 * XY_ROWS + row
            codes[base] = code(kx, ky, kz)
            codes[base + 2 * XY_ROWS] = code(kx, ky, kz)
            if row > 0:
                codes[base + XY_ROWS] = code(-kx, -ky, kz)
                codes[base + 3 * XY_ROWS] = code(-kx, -ky, kz)
        base = TOP * 4 * XY_ROWS + row
        codes[base] = code(kx, ky, 0)
        if row > 0:
            codes[base + XY_ROWS] = code(kx, ky, 0)
    return xy, codes.reshape(ROWS_EACH, DEVICES)


XY, CODES = wave_layout()


def turn_waves(turns):
    rest = turns - jnp.floor(turns + 0.5)
    quarter = rest - 0.25
    quarter = jnp.where(quarter < -0.5, quarter + 1.0, quarter)

    def cosine(part):
        square = part * part
        total = jnp.full_like(square, COS_TERMS[-1])
        for term in COS_TERMS[-2::-1]:
            total = total * square + term
        return total

    return cosine(rest), cosine(quarter)


def table_tile(xy_ref, pos_ref, first, width):
    wide = (XY_ROWS, width)
    coords = [jnp.broadcast_to(pos_ref[d : d + 1, first : first + width], wide) for d in range(2)]
    flat_turns = (
        jnp.broadcast_to(xy_ref[:, 0:1], wide) * coords[0]
        + jnp.broadcast_to(xy_ref[:, 1:2], wide) * coords[1]
    )
    cos_xy, sin_xy = turn_waves(flat_turns)
    steps = lax.broadcasted_iota(jnp.int32, (8, width), 0).astype(jnp.float32)
    cos_z, sin_z = turn_waves(
        steps * jnp.broadcast_to(pos_ref[2:3, first : first + width], (8, width))
    )
    rows = []
    for kz in range(1, TOP + 1):
        cos_k = jnp.broadcast_to(cos_z[kz : kz + 1], wide)
        sin_k = jnp.broadcast_to(sin_z[kz : kz + 1], wide)
        both_cos, both_sin = cos_xy * cos_k, sin_xy * sin_k
        sin_cos, cos_sin = sin_xy * cos_k, cos_xy * sin_k
        rows += [both_cos - both_sin, both_cos + both_sin, cos_sin + sin_cos, cos_sin - sin_cos]
    rows += [cos_xy, sin_xy, jnp.zeros((WAVE_ROWS - 26 * XY_ROWS, width), jnp.float32)]
    return jnp.concatenate(rows, axis=0).astype(jnp.bfloat16)


def hbm():
    return pl.BlockSpec(memory_space=pltpu.HBM)


def vmem():
    return pl.BlockSpec(memory_space=pltpu.VMEM)


def limit(size):
    return pltpu.CompilerParams(vmem_limit_bytes=size)


def loads(sources, targets, arrivals):
    copies = [
        pltpu.make_async_copy(source, target, arrivals.at[at])
        for at, (source, target) in enumerate(zip(sources, targets))
    ]
    for copy in copies:
        copy.start()
    return copies


def factor_kernel(
    count_ref, xy_hbm, pos_hbm, features_hbm, *refs
):
    after_refs, refs = refs[:-6], refs[-6:]
    sums_ref, table_ref, xy_ref, pos_ref, features_ref, arrivals = refs
    del after_refs
    copies = loads((xy_hbm, pos_hbm, features_hbm), (xy_ref, pos_ref, features_ref), arrivals)
    atoms, channels = features_ref.shape
    copies[0].wait()
    copies[1].wait()
    for first in range(0, atoms, 128):
        table_ref[:, first : first + 128] = table_tile(xy_ref, pos_ref, first, 128)
    copies[2].wait()
    live = lax.broadcasted_iota(jnp.int32, (atoms, channels), 0) < count_ref[0]
    masked = jnp.where(live, features_ref[...].astype(jnp.float32), 0.0).astype(jnp.bfloat16)
    for r in range(ROWS_EACH):
        sums_ref[:, r * channels : (r + 1) * channels] = jnp.dot(
            table_ref[r * DEVICES : (r + 1) * DEVICES, :],
            masked,
            preferred_element_type=jnp.float32,
        )


def factor_call(atom_count, positions, features, after):
    atoms, channels = features.shape
    return pl.pallas_call(
        factor_kernel,
        in_specs=[pl.BlockSpec(memory_space=pltpu.SMEM), hbm(), hbm(), hbm()]
        + [pl.BlockSpec(memory_space=pl.ANY)] * len(after),
        out_specs=vmem(),
        out_shape=jax.ShapeDtypeStruct((DEVICES, ROWS_EACH * channels), jnp.float32),
        scratch_shapes=[
            pltpu.VMEM((WAVE_ROWS, atoms), jnp.bfloat16),
            pltpu.VMEM(XY.shape, jnp.float32),
            pltpu.VMEM(positions.shape, jnp.float32),
            pltpu.VMEM(features.shape, jnp.bfloat16),
            pltpu.SemaphoreType.DMA((3,)),
        ],
        compiler_params=limit(LARGE_VMEM),
        name="factor_sums",
    )(atom_count, jnp.asarray(XY), positions, features, *after)


def stage_kernel(sums_ref, out_ref):
    rows = out_ref.shape[1]
    total = sums_ref[0:rows, :]
    for at in range(rows, sums_ref.shape[0], rows):
        total = total + sums_ref[at : at + rows, :]
    for at in range(out_ref.shape[0]):
        out_ref[at] = total


def stage_call(sums, sources, copies):
    return pl.pallas_call(
        stage_kernel,
        out_specs=vmem(),
        out_shape=jax.ShapeDtypeStruct(
            (copies, sums.shape[0] // sources, sums.shape[1]), jnp.float32
        ),
        compiler_params=limit(SMALL_VMEM),
        name="stage_sums",
    )(sums)


def filter_kernel(norm_factor, sums_ref, weight_ref, mix_hbm, out_ref, mix_ref, arrivals):
    copies = loads((mix_hbm,), (mix_ref,), arrivals)
    channels = mix_ref.shape[0]
    total = sums_ref[0]
    for at in range(1, sums_ref.shape[0]):
        total = total + sums_ref[at]
    count = total.shape[0]
    scaled = jnp.concatenate(
        [total[:, r * channels : (r + 1) * channels] for r in range(ROWS_EACH)], axis=0
    )
    scaled = scaled * norm_factor * weight_ref[...]
    copies[0].wait()
    mixed = jnp.dot(
        scaled, mix_ref[...], precision=lax.Precision.HIGHEST, preferred_element_type=jnp.float32
    )
    lines = jnp.concatenate(
        [mixed[r * count : (r + 1) * count] for r in range(ROWS_EACH)], axis=1
    ).astype(jnp.bfloat16)
    for at in range(out_ref.shape[0]):
        out_ref[at] = lines


def filter_call(sums, weights, w_mix, norm_factor, copies):
    return pl.pallas_call(
        functools.partial(filter_kernel, norm_factor),
        in_specs=[vmem(), vmem(), hbm()],
        out_specs=vmem(),
        out_shape=jax.ShapeDtypeStruct((copies,) + sums.shape[1:], jnp.bfloat16),
        scratch_shapes=[pltpu.VMEM(w_mix.shape, jnp.float32), pltpu.SemaphoreType.DMA((1,))],
        compiler_params=limit(SMALL_VMEM),
        name="filter_rows",
    )(sums, weights, w_mix)


def wave_weights(kgrid, k_filter, first, count):
    kx, ky, kz = kgrid[0], kgrid[1], kgrid[2]
    low = (kz < 0) | ((kz == 0) & ((ky < 0) | ((ky == 0) & (kx < 0))))
    sign = jnp.where(low, -1, 1)
    code = ((kz * sign + TOP) * SIDE + ky * sign + TOP) * SIDE + kx * sign + TOP
    mine = lax.dynamic_slice_in_dim(jnp.asarray(CODES), first, count, 1).reshape(-1)
    same = (mine[:, None] == code[None, :]).astype(jnp.float32)
    return jnp.dot(same, k_filter, precision=lax.Precision.HIGHEST)


def receive_kernel(degree, basis_ref, features_ref, recv_ref, wb_ref, after_ref, out_ref, wide_ref):
    atoms, channels = features_ref.shape
    basis_rows = wb_ref.shape[0]
    groups = 128 // basis_rows
    del after_ref

    @pl.when(pl.program_id(0) == 0)
    def _():
        stacked = jnp.concatenate([wb_ref[...].astype(jnp.float32)] * groups, axis=0)
        group_of = lax.broadcasted_iota(jnp.int32, stacked.shape, 0) // basis_rows
        for g in range(groups):
            wide_ref[:, g * channels : (g + 1) * channels] = jnp.where(
                group_of == g, stacked, 0.0
            ).astype(jnp.bfloat16)

    own = jnp.dot(features_ref[...], recv_ref[...], preferred_element_type=jnp.float32)
    values = basis_ref[...].astype(jnp.float32)
    stack = jnp.concatenate([values[:, g * 128 : (g + 1) * 128] for g in range(groups)], axis=0)
    turned = stack.T.astype(jnp.bfloat16)
    each = 128 // degree
    for g in range(0, groups, 2):
        both = jnp.dot(
            turned,
            wide_ref[:, g * channels : (g + 2) * channels],
            preferred_element_type=jnp.float32,
        )
        for side in range(2):
            first = (g + side) * each
            mine = jnp.concatenate(
                [
                    jnp.broadcast_to(own[atom : atom + 1], (degree, channels))
                    for atom in range(first, first + each)
                ],
                axis=0,
            )
            out_ref[(g + side) * 128 : (g + side + 1) * 128, :] = (
                both[:, side * channels : (side + 1) * channels] + mine
            ) * 0.5


def receive_call(features, edge_basis, w_recv, w_basis, after):
    atoms, channels = features.shape
    basis_rows, edges = edge_basis.shape
    degree = edges // atoms
    span = 128 // basis_rows * 128
    whole = lambda array: pl.BlockSpec(array.shape, lambda i: (0, 0))
    return pl.pallas_call(
        functools.partial(receive_kernel, degree),
        grid=(edges // span,),
        in_specs=[
            pl.BlockSpec((basis_rows, span), lambda i: (0, i)),
            pl.BlockSpec((span // degree, channels), lambda i: (i, 0)),
            whole(w_recv),
            whole(w_basis),
            pl.BlockSpec(memory_space=pl.ANY),
        ],
        out_specs=pl.BlockSpec((span, channels), lambda i: (i, 0)),
        out_shape=jax.ShapeDtypeStruct((edges, channels), jnp.float32),
        scratch_shapes=[pltpu.VMEM((128, 128 // basis_rows * channels), jnp.bfloat16)],
        compiler_params=limit(TABLE_VMEM),
        cost_estimate=pl.CostEstimate(
            flops=5 * 10**9, bytes_accessed=18 * 10**6, transcendentals=0
        ),
        name="receive_rows",
    )(edge_basis, features, w_recv, w_basis, after)


def edge_kernel(degree, first, ids_hbm, base_hbm, wo_hbm, *refs):
    blocks, refs = refs[:7], refs[7:]
    (after_ref, out_ref, pool_ref, part_ref, base_ref, ids_ref, wo_ref), refs = refs[:7], refs[7:]
    loaded, streamed, refs = refs[0], refs[1], refs[2:]
    buffers, arrivals = refs[:BUFFERS], refs[BUFFERS:]
    atoms, channels = out_ref.shape
    del after_ref
    edges = UNROLL * degree
    lines = edges // 128
    chunks = atoms // UNROLL
    rounds = chunks // BUFFERS
    span = edges * BUFFERS
    copies = loads(
        (ids_hbm.at[pl.ds(first * degree // 128, atoms * degree // 128), :], wo_hbm),
        (ids_ref, wo_ref),
        loaded,
    )

    def stream(step):
        slot = lax.rem(step, 2)
        start = pl.multiple_of(first * degree + step * span, span)
        return pltpu.make_async_copy(
            base_hbm.at[pl.ds(start, span), :], base_ref.at[slot], streamed.at[slot]
        )

    def fetch(chunk, at):
        source = ids_ref.at[pl.ds(chunk * lines, lines), :]
        return pltpu.make_async_copy(source, buffers[at], arrivals[at])

    stream(0).start()
    slab_even = lax.rem(lax.axis_index("slab"), 2) == 0
    sub_even = lax.rem(lax.axis_index("sub"), 2) == 0
    slab_place = (1, jnp.where(slab_even, 2, 0), jnp.where(slab_even, 0, 2))
    sub_place = (1, jnp.where(sub_even, 2, 0), jnp.where(sub_even, 0, 2))
    for copy in copies:
        copy.wait()
    for at in range(BUFFERS):
        fetch(at, at).start()
    rows = blocks[0].shape[0]
    at = 0
    for block in blocks:
        for first_row in range(0, block.shape[0], rows):
            place = pl.multiple_of((slab_place[at // 3] * 3 + sub_place[at % 3]) * rows, rows)
            pool_ref[pl.ds(place, rows), :] = (
                block[first_row : first_row + rows, :].astype(jnp.float32) * 0.5
            )
            at += 1

    sublane = lax.broadcasted_iota(jnp.int32, (8, channels), 0)
    at_sublane = [sublane == r for r in range(8)]

    def some_atoms(chunk, ids, base):
        part = part_ref.at[pl.ds(pl.multiple_of(chunk * UNROLL * 8, UNROLL * 8), UNROLL * 8), :]
        for u in range(UNROLL):
            total = None
            for edge in range(u * degree, (u + 1) * degree, 8):
                sent = None
                for r in range(8):
                    sender = ids[(edge + r) // 128, (edge + r) % 128]
                    row = jnp.broadcast_to(pool_ref[pl.ds(sender, 1), :], (8, channels))
                    sent = row if sent is None else jnp.where(at_sublane[r], row, sent)
                half = sent + base[edge : edge + 8, :]
                hidden = (half + half * jnp.tanh(half)).astype(jnp.bfloat16).astype(jnp.float32)
                total = hidden if total is None else total + hidden
            part[u * 8 : u * 8 + 8, :] = total

    def round_of_chunks(step, carry):
        stream(step).wait()

        @pl.when(step + 1 < rounds)
        def _():
            stream(step + 1).start()

        slot = base_ref.at[lax.rem(step, 2)]
        for at in range(BUFFERS):
            chunk = step * BUFFERS + at
            fetch(chunk, at).wait()
            some_atoms(chunk, buffers[at], slot.at[pl.ds(at * edges, edges), :])
            fetch(jnp.minimum(chunk + BUFFERS, chunks - 1), at).start()
        return carry

    lax.fori_loop(0, rounds, round_of_chunks, 0)
    for at in range(BUFFERS):
        fetch(chunks - 1, at).wait()
    summed = part_ref[pl.ds(0, atoms, stride=8), :]
    for r in range(1, 8):
        summed = summed + part_ref[pl.ds(r, atoms, stride=8), :]
    high = summed.astype(jnp.bfloat16)
    low = (summed - high.astype(jnp.float32)).astype(jnp.bfloat16)
    message = jnp.dot(high, wo_ref[...], preferred_element_type=jnp.float32) + jnp.dot(
        low, wo_ref[...], preferred_element_type=jnp.float32
    )
    out_ref[...] = message * (1.0 / math.sqrt(degree))


def edge_call(part, after, senders, base, w_out, blocks):
    channels = base.shape[1]
    degree = base.shape[0] // blocks[0].shape[0]
    atoms, first = PARTS[part], sum(PARTS[:part])
    rows = sum(block.shape[0] for block in blocks)
    return pl.pallas_call(
        functools.partial(edge_kernel, degree, first),
        in_specs=[hbm()] * 3 + [vmem()] * len(blocks) + [pl.BlockSpec(memory_space=pl.ANY)],
        out_specs=vmem(),
        out_shape=jax.ShapeDtypeStruct((atoms, channels), jnp.float32),
        scratch_shapes=[
            pltpu.VMEM((rows, channels), jnp.float32),
            pltpu.VMEM((atoms * 8, channels), jnp.float32),
            pltpu.VMEM((2, UNROLL * BUFFERS * degree, channels), jnp.float32),
            pltpu.VMEM((atoms * degree // 128, 128), jnp.int32),
            pltpu.VMEM(w_out.shape, jnp.bfloat16),
            pltpu.SemaphoreType.DMA((2,)),
            pltpu.SemaphoreType.DMA((2,)),
        ]
        + [pltpu.SMEM((UNROLL * degree // 128, 128), jnp.int32)] * BUFFERS
        + [pltpu.SemaphoreType.DMA] * BUFFERS,
        compiler_params=limit(LARGE_VMEM),
        cost_estimate=pl.CostEstimate(
            flops=12 * 10**9, bytes_accessed=12 * 10**6, transcendentals=2 * 10**6
        ),
        name="edge_part_%d" % part,
    )(senders.reshape(-1, 128), base, w_out, *blocks, after)


def final_kernel(scale, count_ref, xy_hbm, pos_hbm, factors_ref, *refs):
    parts, (out_ref, xy_ref, pos_ref, arrivals) = refs[:-4], refs[-4:]
    copies = loads((xy_hbm, pos_hbm), (xy_ref, pos_ref), arrivals)
    channels = out_ref.shape[1]
    factors = jnp.concatenate(
        [factors_ref[:, r * channels : (r + 1) * channels] for r in range(ROWS_EACH)], axis=0
    ).T
    total, first = out_ref.shape[0], 0
    for part in parts:
        out_ref[first : first + part.shape[0], :] = part[...]
        first += part.shape[0]
    for copy in copies:
        copy.wait()
    atoms = 256
    for first in range(0, total, atoms):
        table = table_tile(xy_ref, pos_ref, first, atoms)
        field = jnp.dot(factors, table, preferred_element_type=jnp.float32)
        live = first + lax.broadcasted_iota(jnp.int32, (atoms, channels), 0) < count_ref[0]
        near = out_ref[first : first + atoms, :]
        out_ref[first : first + atoms, :] = jnp.where(live, near + field.T * scale, 0.0)


def final_call(atom_count, positions, factors, parts, scale):
    atoms = sum(part.shape[0] for part in parts)
    channels = parts[0].shape[1]
    return pl.pallas_call(
        functools.partial(final_kernel, scale),
        in_specs=[pl.BlockSpec(memory_space=pltpu.SMEM), hbm(), hbm(), vmem()]
        + [vmem()] * len(parts),
        out_specs=vmem(),
        out_shape=jax.ShapeDtypeStruct((atoms, channels), jnp.float32),
        scratch_shapes=[
            pltpu.VMEM(XY.shape, jnp.float32),
            pltpu.VMEM(positions.shape, jnp.float32),
            pltpu.SemaphoreType.DMA((2,)),
        ],
        compiler_params=limit(TABLE_VMEM),
        name="updated_rows",
    )(atom_count, jnp.asarray(XY), positions, factors, *parts)


def moved(array, target):
    slabs, subs = lax.axis_size("slab"), lax.axis_size("sub")
    pairs = []
    for s in range(slabs):
        for b in range(subs):
            to_s, to_b = target(s, b)
            pairs.append((s * subs + b, to_s % slabs * subs + to_b % subs))
    return lax.ppermute(array, ("slab", "sub"), pairs)


def to_core(s, b):
    return s ^ 1, b


def to_outer(s, b):
    return s + (1 if s % 2 else -1), b


def to_column(s, b):
    return s, b ^ 1


def to_beyond(s, b):
    return s, b + (-1 if b % 2 == 0 else 1)


def plane_groups(slabs, subs):
    return [
        [(z * PLANE + q) * subs + b for b in range(subs) for q in range(PLANE)]
        for z in range(slabs // PLANE)
    ]


def line_groups(slabs, subs):
    return [
        [(z * PLANE + q) * subs + b for z in range(slabs // PLANE)]
        for b in range(subs)
        for q in range(PLANE)
    ]


def exchanged(array, groups):
    return lax.all_to_all(array, ("slab", "sub"), 0, 0, axis_index_groups=groups, tiled=True)


def per_device(
    features, positions, atom_count, kgrid, k_filter, w_mix, w_recv, w_send, w_basis, w_out,
    edge_basis, senders,
):
    atoms, channels = features.shape
    total_k = kgrid.shape[1]
    subs, slabs = lax.axis_size("sub"), lax.axis_size("slab")
    send_proj = jnp.dot(features, w_send, preferred_element_type=jnp.float32).astype(jnp.bfloat16)
    outer = moved(send_proj, to_outer)
    near = moved(send_proj, to_column)
    beyond = moved(send_proj, to_beyond)
    outer_near = moved(send_proj, lambda s, b: to_outer(*to_column(s, b)))
    outer_beyond = moved(send_proj, lambda s, b: to_outer(*to_beyond(s, b)))
    core = moved(jnp.concatenate([send_proj, near, beyond]), to_core)
    blocks = [send_proj, near, beyond, core, outer, outer_near, outer_beyond]

    plane, line = plane_groups(slabs, subs), line_groups(slabs, subs)
    mine = lax.axis_index("sub") * PLANE + lax.axis_index("slab") % PLANE
    sums = factor_call(atom_count, positions, features, ())
    stage_one = stage_call(exchanged(sums, plane), len(plane[0]), len(line[0]))
    count = stage_one.shape[1]
    weights = wave_weights(kgrid, k_filter, mine * count, count)
    norm_factor = 1.0 / math.sqrt(atoms * DEVICES)
    filtered = filter_call(
        exchanged(stage_one, line), weights, w_mix, norm_factor, len(plane[0])
    )
    factors = exchanged(filtered, plane).reshape(DEVICES, -1)

    base = receive_call(features, edge_basis, w_recv, w_basis, sums)
    after = [stage_one, filtered]
    parts = [
        edge_call(p, after[p], senders, base, w_out, blocks) for p in range(len(PARTS))
    ]
    return final_call(atom_count, positions, factors, parts, 4.0 / math.sqrt(total_k))


def solution(mesh):
    placed = (
        P(("slab", "sub"), None),
        P(None, ("slab", "sub")),
        P(("slab", "sub")),
        P(), P(), P(), P(), P(), P(), P(),
        P(None, ("slab", "sub")),
        P(("slab", "sub")),
    )
    return jax.shard_map(
        per_device, mesh=mesh, in_specs=placed, out_specs=P(("slab", "sub"), None), check_vma=False
    )
```

```python
import functools
import math

import jax
import jax.numpy as jnp
import numpy as np
from jax import lax
from jax.experimental import pallas as pl
from jax.experimental.pallas import tpu as pltpu
from jax.sharding import PartitionSpec as P

TOP = 6
SIDE = 2 * TOP + 1
XY_ROWS = 88
WAVE_ROWS = 2304
DEVICES = 256
ROWS_EACH = WAVE_ROWS // DEVICES
HALF_ROWS = WAVE_ROWS // 2
HALF_TOP = TOP // 2
PARTS = (512, 512)
PLANE = 4
UNROLL = 16
BUFFERS = 4
COS_TERMS = (
    0.999999989059022, -19.7392044994538, 64.93911745989, -85.4501395308031,
    60.1676309503793, -25.9675992464965, 6.52865815867317,
)
SMALL_VMEM, TABLE_VMEM, LARGE_VMEM = 6 * 2**20, 14 * 2**20, 60 * 2**20


def wave_layout():
    flat = [(0, 0)] + [(kx, 0) for kx in range(1, TOP + 1)]
    flat += [(kx, ky) for ky in range(1, TOP + 1) for kx in range(-TOP, TOP + 1)]
    codes = np.full((2, HALF_ROWS), -1, np.int32)
    xy = np.zeros((XY_ROWS, 2), np.float32)

    def code(kx, ky, kz):
        return ((kz + TOP) * SIDE + ky + TOP) * SIDE + kx + TOP

    for row, (kx, ky) in enumerate(flat):
        xy[row] = kx, ky
        for kz in range(1, TOP + 1):
            half, at = divmod(kz - 1, HALF_TOP)
            base = at * 4 * XY_ROWS + row
            codes[half, base] = code(kx, ky, kz)
            codes[half, base + 2 * XY_ROWS] = code(kx, ky, kz)
            if row > 0:
                codes[half, base + XY_ROWS] = code(-kx, -ky, kz)
                codes[half, base + 3 * XY_ROWS] = code(-kx, -ky, kz)
        base = HALF_TOP * 4 * XY_ROWS + row
        codes[0, base] = code(kx, ky, 0)
        if row > 0:
            codes[1, base] = code(kx, ky, 0)
    each = DEVICES // 2
    codes = codes.reshape(2, ROWS_EACH, each).transpose(1, 0, 2)
    return xy, codes.reshape(ROWS_EACH, DEVICES)


XY, CODES = wave_layout()


def turn_waves(turns):
    rest = turns - jnp.floor(turns + 0.5)
    quarter = rest - 0.25
    quarter = jnp.where(quarter < -0.5, quarter + 1.0, quarter)

    def cosine(part):
        square = part * part
        total = jnp.full_like(square, COS_TERMS[-1])
        for term in COS_TERMS[-2::-1]:
            total = total * square + term
        return total

    return cosine(rest), cosine(quarter)


def flat_waves(xy_ref, pos_ref, first, width):
    wide = (XY_ROWS, width)
    coords = [jnp.broadcast_to(pos_ref[d : d + 1, first : first + width], wide) for d in range(2)]
    flat_turns = (
        jnp.broadcast_to(xy_ref[:, 0:1], wide) * coords[0]
        + jnp.broadcast_to(xy_ref[:, 1:2], wide) * coords[1]
    )
    return turn_waves(flat_turns)


def half_table(flat, pos_ref, first, half):
    cos_xy, sin_xy = flat
    wide = cos_xy.shape
    width = wide[1]
    steps = lax.broadcasted_iota(jnp.int32, (8, width), 0) + (1 + HALF_TOP * half)
    cos_z, sin_z = turn_waves(
        steps.astype(jnp.float32)
        * jnp.broadcast_to(pos_ref[2:3, first : first + width], (8, width))
    )
    rows = []
    for at in range(HALF_TOP):
        cos_k = jnp.broadcast_to(cos_z[at : at + 1], wide)
        sin_k = jnp.broadcast_to(sin_z[at : at + 1], wide)
        both_cos, both_sin = cos_xy * cos_k, sin_xy * sin_k
        sin_cos, cos_sin = sin_xy * cos_k, cos_xy * sin_k
        rows += [both_cos - both_sin, both_cos + both_sin, cos_sin + sin_cos, cos_sin - sin_cos]
    rows.append(jnp.where(half == 0, cos_xy, sin_xy))
    rows.append(jnp.zeros((HALF_ROWS - (4 * HALF_TOP + 1) * XY_ROWS, width), jnp.float32))
    return jnp.concatenate(rows, axis=0).astype(jnp.bfloat16)


def hbm():
    return pl.BlockSpec(memory_space=pltpu.HBM)


def vmem():
    return pl.BlockSpec(memory_space=pltpu.VMEM)


def limit(size):
    return pltpu.CompilerParams(vmem_limit_bytes=size)


def loads(sources, targets, arrivals):
    copies = [
        pltpu.make_async_copy(source, target, arrivals.at[at])
        for at, (source, target) in enumerate(zip(sources, targets))
    ]
    for copy in copies:
        copy.start()
    return copies


def packed_rows(atoms):
    return 3 * 8 * atoms // 128


def prepare_kernel(count_ref, pos_hbm, features_hbm, packed_ref, *refs):
    pos_ref, features_ref, wide_ref, arrivals = refs
    copies = loads((pos_hbm, features_hbm), (pos_ref, features_ref), arrivals)
    atoms, channels = features_ref.shape
    wide_ref[...] = jnp.zeros_like(wide_ref)
    for copy in copies:
        copy.wait()
    live = lax.broadcasted_iota(jnp.int32, (atoms, channels), 0) < count_ref[0]
    masked = jnp.where(live, features_ref[...].astype(jnp.float32), 0.0).astype(jnp.bfloat16)
    packed_ref[0:atoms, :] = masked
    wide_ref[0:3, :] = pos_ref[...]
    rest = wide_ref[...]
    pieces = []
    for _ in range(3):
        piece = rest.astype(jnp.bfloat16).astype(jnp.float32)
        rest = rest - piece
        pieces += [piece[:, at : at + 128] for at in range(0, atoms, 128)]
    packed_ref[atoms:, :] = jnp.concatenate(pieces, axis=0).astype(jnp.bfloat16)


def prepare_call(atom_count, positions, features):
    atoms, channels = features.shape
    return pl.pallas_call(
        prepare_kernel,
        in_specs=[pl.BlockSpec(memory_space=pltpu.SMEM), hbm(), hbm()],
        out_specs=vmem(),
        out_shape=jax.ShapeDtypeStruct((atoms + packed_rows(atoms), channels), jnp.bfloat16),
        scratch_shapes=[
            pltpu.VMEM(positions.shape, jnp.float32),
            pltpu.VMEM(features.shape, jnp.bfloat16),
            pltpu.VMEM((8, atoms), jnp.float32),
            pltpu.SemaphoreType.DMA((2,)),
        ],
        compiler_params=limit(SMALL_VMEM),
        name="prepare_rows",
    )(atom_count, positions, features)


def project_kernel(packed_ref, send_ref, after_ref, out_ref):
    del after_ref
    rows = packed_ref[0 : out_ref.shape[0], :]
    out_ref[...] = jnp.dot(rows, send_ref[...], preferred_element_type=jnp.float32).astype(
        jnp.bfloat16
    )


def project_call(packed, w_send, atoms, after):
    return pl.pallas_call(
        project_kernel,
        in_specs=[vmem(), vmem(), pl.BlockSpec(memory_space=pl.ANY)],
        out_specs=vmem(),
        out_shape=jax.ShapeDtypeStruct((atoms, w_send.shape[1]), jnp.bfloat16),
        compiler_params=limit(SMALL_VMEM),
        name="project_rows",
    )(packed, w_send, after)


def factor_kernel(xy_hbm, packed_any, other_any, *refs):
    sums_ref, table_ref, xy_ref, packed_ref, pos_ref, arrivals = refs
    copies = loads(
        (xy_hbm, packed_any, other_any), (xy_ref, packed_ref.at[0], packed_ref.at[1]), arrivals
    )
    half = lax.rem(lax.axis_index("slab"), 2)
    atoms = pos_ref.shape[1]
    channels = packed_ref.shape[2]
    for copy in copies:
        copy.wait()
    tiles = atoms // 128
    for side in range(2):
        values = packed_ref[side, atoms:, :].astype(jnp.float32)
        for at in range(tiles):
            total = None
            for piece in range(3):
                start = (piece * tiles + at) * 8
                part = values[start : start + 8]
                total = part if total is None else total + part
            pos_ref[:, at * 128 : (at + 1) * 128] = total
        for first in range(0, atoms, 128):
            table_ref[:, side * atoms + first : side * atoms + first + 128] = half_table(
                flat_waves(xy_ref, pos_ref, first, 128), pos_ref, first, half
            )
    each = sums_ref.shape[0]
    for r in range(ROWS_EACH):
        rows = table_ref[r * each : (r + 1) * each, :]
        sums_ref[:, r * channels : (r + 1) * channels] = jnp.dot(
            rows[:, :atoms], packed_ref[0, :atoms, :], preferred_element_type=jnp.float32
        ) + jnp.dot(
            rows[:, atoms:], packed_ref[1, :atoms, :], preferred_element_type=jnp.float32
        )


def factor_call(packed, other, atoms):
    channels = packed.shape[1]
    anywhere = pl.BlockSpec(memory_space=pl.ANY)
    return pl.pallas_call(
        factor_kernel,
        in_specs=[hbm(), anywhere, anywhere],
        out_specs=vmem(),
        out_shape=jax.ShapeDtypeStruct((DEVICES // 2, ROWS_EACH * channels), jnp.float32),
        scratch_shapes=[
            pltpu.VMEM((HALF_ROWS, 2 * atoms), jnp.bfloat16),
            pltpu.VMEM(XY.shape, jnp.float32),
            pltpu.VMEM((2,) + packed.shape, jnp.bfloat16),
            pltpu.VMEM((8, atoms), jnp.float32),
            pltpu.SemaphoreType.DMA((3,)),
        ],
        compiler_params=limit(TABLE_VMEM),
        name="factor_sums",
    )(jnp.asarray(XY), packed, other)


def stage_kernel(sums_ref, out_ref):
    rows = out_ref.shape[1]
    total = sums_ref[0:rows, :]
    for at in range(rows, sums_ref.shape[0], rows):
        total = total + sums_ref[at : at + rows, :]
    for at in range(out_ref.shape[0]):
        out_ref[at] = total


def stage_call(sums, sources, copies):
    return pl.pallas_call(
        stage_kernel,
        out_specs=vmem(),
        out_shape=jax.ShapeDtypeStruct(
            (copies, sums.shape[0] // sources, sums.shape[1]), jnp.float32
        ),
        compiler_params=limit(SMALL_VMEM),
        name="stage_sums",
    )(sums)


def filter_kernel(norm_factor, sums_ref, weight_ref, mix_hbm, out_ref, mix_ref, arrivals):
    copies = loads((mix_hbm,), (mix_ref,), arrivals)
    channels = mix_ref.shape[0]
    total = sums_ref[0]
    for at in range(1, sums_ref.shape[0]):
        total = total + sums_ref[at]
    count = total.shape[0]
    scaled = jnp.concatenate(
        [total[:, r * channels : (r + 1) * channels] for r in range(ROWS_EACH)], axis=0
    )
    scaled = scaled * norm_factor * weight_ref[...]
    copies[0].wait()
    mixed = jnp.dot(
        scaled, mix_ref[...], precision=lax.Precision.HIGHEST, preferred_element_type=jnp.float32
    )
    lines = jnp.concatenate(
        [mixed[r * count : (r + 1) * count] for r in range(ROWS_EACH)], axis=1
    ).astype(jnp.bfloat16)
    for at in range(out_ref.shape[0]):
        out_ref[at] = lines


def filter_call(sums, weights, w_mix, norm_factor, copies):
    return pl.pallas_call(
        functools.partial(filter_kernel, norm_factor),
        in_specs=[vmem(), vmem(), hbm()],
        out_specs=vmem(),
        out_shape=jax.ShapeDtypeStruct((copies,) + sums.shape[1:], jnp.bfloat16),
        scratch_shapes=[pltpu.VMEM(w_mix.shape, jnp.float32), pltpu.SemaphoreType.DMA((1,))],
        compiler_params=limit(SMALL_VMEM),
        name="filter_rows",
    )(sums, weights, w_mix)


def wave_weights(kgrid, k_filter, first, count):
    kx, ky, kz = kgrid[0], kgrid[1], kgrid[2]
    low = (kz < 0) | ((kz == 0) & ((ky < 0) | ((ky == 0) & (kx < 0))))
    sign = jnp.where(low, -1, 1)
    code = ((kz * sign + TOP) * SIDE + ky * sign + TOP) * SIDE + kx * sign + TOP
    mine = lax.dynamic_slice_in_dim(jnp.asarray(CODES), first, count, 1).reshape(-1)
    same = (mine[:, None] == code[None, :]).astype(jnp.float32)
    return jnp.dot(same, k_filter, precision=lax.Precision.HIGHEST)


def edge_kernel(
    degree, first, ids_hbm, basis_hbm, features_hbm, recv_hbm, wb_hbm, wo_hbm, *refs
):
    blocks, refs = refs[:7], refs[7:]
    (after_ref, out_ref, pool_ref, radial_ref, part_ref, own_ref, wide_ref), refs = refs[:7], refs[7:]
    local, held, loaded, landed, refs = refs[:6], refs[6:13], refs[13], refs[14], refs[15:]
    ids_ref, basis_ref, features_ref, recv_ref, wb_ref, wo_ref = local
    buffers, arrivals = refs[:BUFFERS], refs[BUFFERS:]
    atoms, channels = out_ref.shape
    del after_ref
    copies = loads(
        (
            ids_hbm.at[pl.ds(first * degree // 128, atoms * degree // 128), :],
            basis_hbm.at[:, pl.ds(first * degree, atoms * degree)],
            features_hbm.at[pl.ds(first, atoms), :],
            recv_hbm,
            wb_hbm,
            wo_hbm,
        ),
        local,
        loaded,
    )
    landing = loads(blocks, held, landed)
    edges = UNROLL * degree
    lines = edges // 128
    chunks = atoms // UNROLL

    def fetch(chunk, at):
        source = ids_ref.at[pl.ds(chunk * lines, lines), :]
        return pltpu.make_async_copy(source, buffers[at], arrivals[at])

    slab_even = lax.rem(lax.axis_index("slab"), 2) == 0
    sub_even = lax.rem(lax.axis_index("sub"), 2) == 0
    slab_place = (1, jnp.where(slab_even, 2, 0), jnp.where(slab_even, 0, 2))
    sub_place = (1, jnp.where(sub_even, 2, 0), jnp.where(sub_even, 0, 2))
    for copy in copies:
        copy.wait()
    for at in range(BUFFERS):
        fetch(at, at).start()
    own_ref[...] = jnp.dot(features_ref[...], recv_ref[...], preferred_element_type=jnp.float32)

    basis_rows = wb_ref.shape[0]
    groups = 128 // basis_rows
    stacked = jnp.concatenate([wb_ref[...].astype(jnp.float32)] * groups, axis=0)
    group_of = lax.broadcasted_iota(jnp.int32, stacked.shape, 0) // basis_rows
    for g in range(groups):
        wide_ref[:, g * channels : (g + 1) * channels] = jnp.where(
            group_of == g, stacked, 0.0
        ).astype(jnp.bfloat16)

    span = groups * 128

    def radial_block(step, carry):
        turned = []
        for at in range(2):
            values = basis_ref[:, pl.ds(pl.multiple_of((step * 2 + at) * span, span), span)]
            values = values.astype(jnp.float32)
            stack = jnp.concatenate(
                [values[:, g * 128 : (g + 1) * 128] for g in range(groups)], axis=0
            )
            turned.append(stack.T.astype(jnp.bfloat16))
        turned = jnp.concatenate(turned, axis=0)
        for g in range(0, groups, 2):
            both = jnp.dot(
                turned,
                wide_ref[:, g * channels : (g + 2) * channels],
                preferred_element_type=jnp.float32,
            )
            for at in range(2):
                base = pl.multiple_of((step * 2 + at) * span, span) + g * 128
                half = both[at * 128 : (at + 1) * 128]
                radial_ref[pl.ds(base, 128), :] = half[:, :channels]
                radial_ref[pl.ds(base + 128, 128), :] = half[:, channels:]
        return carry

    lax.fori_loop(0, atoms * degree // span // 2, radial_block, 0)
    rows = blocks[0].shape[0]
    at = 0
    for copy, block in zip(landing, held):
        copy.wait()
        for first_row in range(0, block.shape[0], rows):
            place = pl.multiple_of((slab_place[at // 3] * 3 + sub_place[at % 3]) * rows, rows)
            pool_ref[pl.ds(place, rows), :] = block[first_row : first_row + rows, :].astype(
                jnp.float32
            )
            at += 1

    sublane = lax.broadcasted_iota(jnp.int32, (8, channels), 0)
    at_sublane = [sublane == r for r in range(8)]

    def some_atoms(chunk, ids):
        own = own_ref.at[pl.ds(pl.multiple_of(chunk * UNROLL, UNROLL), UNROLL), :]
        part = part_ref.at[pl.ds(pl.multiple_of(chunk * UNROLL * 8, UNROLL * 8), UNROLL * 8), :]
        radial = radial_ref.at[pl.ds(pl.multiple_of(chunk * edges, edges), edges), :]
        for u in range(UNROLL):
            mine = jnp.broadcast_to(own[u : u + 1, :], (8, channels))
            total = None
            for edge in range(u * degree, (u + 1) * degree, 8):
                sent = None
                for r in range(8):
                    sender = ids[(edge + r) // 128, (edge + r) % 128]
                    row = jnp.broadcast_to(pool_ref[pl.ds(sender, 1), :], (8, channels))
                    sent = row if sent is None else jnp.where(at_sublane[r], row, sent)
                half = (sent + radial[edge : edge + 8, :] + mine) * 0.5
                hidden = (half + half * jnp.tanh(half)).astype(jnp.bfloat16).astype(jnp.float32)
                total = hidden if total is None else total + hidden
            part[u * 8 : u * 8 + 8, :] = total

    def round_of_chunks(step, carry):
        for at in range(BUFFERS):
            chunk = step * BUFFERS + at
            fetch(chunk, at).wait()
            some_atoms(chunk, buffers[at])
            fetch(jnp.minimum(chunk + BUFFERS, chunks - 1), at).start()
        return carry

    lax.fori_loop(0, chunks // BUFFERS, round_of_chunks, 0)
    for at in range(BUFFERS):
        fetch(chunks - 1, at).wait()
    summed = part_ref[pl.ds(0, atoms, stride=8), :]
    for r in range(1, 8):
        summed = summed + part_ref[pl.ds(r, atoms, stride=8), :]
    high = summed.astype(jnp.bfloat16)
    low = (summed - high.astype(jnp.float32)).astype(jnp.bfloat16)
    message = jnp.dot(high, wo_ref[...], preferred_element_type=jnp.float32) + jnp.dot(
        low, wo_ref[...], preferred_element_type=jnp.float32
    )
    out_ref[...] = message * (1.0 / math.sqrt(degree))


def edge_call(part, after, senders, edge_basis, features, w_recv, w_basis, w_out, blocks):
    channels = features.shape[1]
    degree = senders.shape[0] // features.shape[0]
    atoms, first = PARTS[part], sum(PARTS[:part])
    rows = sum(block.shape[0] for block in blocks)
    return pl.pallas_call(
        functools.partial(edge_kernel, degree, first),
        in_specs=[hbm()] * 6 + [pl.BlockSpec(memory_space=pl.ANY)] * (len(blocks) + 1),
        out_specs=vmem(),
        out_shape=jax.ShapeDtypeStruct((atoms, channels), jnp.float32),
        scratch_shapes=[
            pltpu.VMEM((rows, channels), jnp.float32),
            pltpu.VMEM((atoms * degree, channels), jnp.float32),
            pltpu.VMEM((atoms * 8, channels), jnp.float32),
            pltpu.VMEM((atoms, channels), jnp.float32),
            pltpu.VMEM((128, 128 // w_basis.shape[0] * channels), jnp.bfloat16),
            pltpu.VMEM((atoms * degree // 128, 128), jnp.int32),
            pltpu.VMEM((edge_basis.shape[0], atoms * degree), jnp.bfloat16),
            pltpu.VMEM((atoms, channels), jnp.bfloat16),
            pltpu.VMEM(w_recv.shape, jnp.bfloat16),
            pltpu.VMEM(w_basis.shape, jnp.bfloat16),
            pltpu.VMEM(w_out.shape, jnp.bfloat16),
        ]
        + [pltpu.VMEM(block.shape, jnp.bfloat16) for block in blocks]
        + [pltpu.SemaphoreType.DMA((6,)), pltpu.SemaphoreType.DMA((len(blocks),))]
        + [pltpu.SMEM((UNROLL * degree // 128, 128), jnp.int32)] * BUFFERS
        + [pltpu.SemaphoreType.DMA] * BUFFERS,
        compiler_params=limit(LARGE_VMEM),
        cost_estimate=pl.CostEstimate(
            flops=8 * 10**9, bytes_accessed=4 * 10**6, transcendentals=10**6
        ),
        name="edge_part_%d" % part,
    )(
        senders.reshape(-1, 128), edge_basis, features, w_recv, w_basis, w_out, *blocks, after
    )


def final_kernel(scale, count_ref, xy_hbm, pos_hbm, factors_ref, *refs):
    parts, (out_ref, xy_ref, pos_ref, arrivals) = refs[:-4], refs[-4:]
    copies = loads((xy_hbm, pos_hbm), (xy_ref, pos_ref), arrivals)
    channels = out_ref.shape[1]
    each = DEVICES // 2
    factors = jnp.concatenate(
        [
            factors_ref[half * each : (half + 1) * each, r * channels : (r + 1) * channels]
            for half in range(2)
            for r in range(ROWS_EACH)
        ],
        axis=0,
    ).T
    total, first = out_ref.shape[0], 0
    for part in parts:
        out_ref[first : first + part.shape[0], :] = part[...]
        first += part.shape[0]
    for copy in copies:
        copy.wait()
    atoms = 256
    for first in range(0, total, atoms):
        flat = flat_waves(xy_ref, pos_ref, first, atoms)
        table = jnp.concatenate(
            [half_table(flat, pos_ref, first, half) for half in range(2)], axis=0
        )
        field = jnp.dot(factors, table, preferred_element_type=jnp.float32)
        live = first + lax.broadcasted_iota(jnp.int32, (atoms, channels), 0) < count_ref[0]
        near = out_ref[first : first + atoms, :]
        out_ref[first : first + atoms, :] = jnp.where(live, near + field.T * scale, 0.0)


def final_call(atom_count, positions, factors, parts, scale):
    atoms = sum(part.shape[0] for part in parts)
    channels = parts[0].shape[1]
    return pl.pallas_call(
        functools.partial(final_kernel, scale),
        in_specs=[pl.BlockSpec(memory_space=pltpu.SMEM), hbm(), hbm(), vmem()]
        + [vmem()] * len(parts),
        out_specs=vmem(),
        out_shape=jax.ShapeDtypeStruct((atoms, channels), jnp.float32),
        scratch_shapes=[
            pltpu.VMEM(XY.shape, jnp.float32),
            pltpu.VMEM(positions.shape, jnp.float32),
            pltpu.SemaphoreType.DMA((2,)),
        ],
        compiler_params=limit(TABLE_VMEM),
        name="updated_rows",
    )(atom_count, jnp.asarray(XY), positions, factors, *parts)


def column_kernel(own_ref, near_ref, beyond_ref, after_ref, out_ref):
    del after_ref
    rows = own_ref.shape[0]
    for at, block in enumerate((own_ref, near_ref, beyond_ref)):
        out_ref[at * rows : (at + 1) * rows, :] = block[...]


def column_call(blocks, after):
    rows, channels = blocks[0].shape
    return pl.pallas_call(
        column_kernel,
        in_specs=[vmem()] * 3 + [pl.BlockSpec(memory_space=pl.ANY)],
        out_specs=vmem(),
        out_shape=jax.ShapeDtypeStruct((3 * rows, channels), blocks[0].dtype),
        compiler_params=limit(SMALL_VMEM),
        name="column_rows",
    )(*blocks, after)


def moved(array, target):
    slabs, subs = lax.axis_size("slab"), lax.axis_size("sub")
    pairs = []
    for s in range(slabs):
        for b in range(subs):
            to_s, to_b = target(s, b)
            pairs.append((s * subs + b, to_s % slabs * subs + to_b % subs))
    return lax.ppermute(array, ("slab", "sub"), pairs)


def to_core(s, b):
    return s ^ 1, b


def to_outer(s, b):
    return s + (1 if s % 2 else -1), b


def to_column(s, b):
    return s, b ^ 1


def to_beyond(s, b):
    return s, b + (-1 if b % 2 == 0 else 1)


def plane_groups(slabs, subs):
    return [
        [
            (z * PLANE + 2 * q + core) * subs + b
            for core in range(2)
            for b in range(subs)
            for q in range(PLANE // 2)
        ]
        for z in range(slabs // PLANE)
    ]


def core_groups(slabs, subs):
    planes = plane_groups(slabs, subs)
    half = len(planes[0]) // 2
    return [group[core * half : (core + 1) * half] for group in planes for core in range(2)]


def line_groups(slabs, subs):
    return [
        [(z * PLANE + q) * subs + b for z in range(slabs // PLANE)]
        for b in range(subs)
        for q in range(PLANE)
    ]


def exchanged(array, groups):
    return lax.all_to_all(array, ("slab", "sub"), 0, 0, axis_index_groups=groups, tiled=True)


def per_device(
    features, positions, atom_count, kgrid, k_filter, w_mix, w_recv, w_send, w_basis, w_out,
    edge_basis, senders,
):
    atoms, channels = features.shape
    total_k = kgrid.shape[1]
    subs, slabs = lax.axis_size("sub"), lax.axis_size("slab")
    packed = prepare_call(atom_count, positions, features)
    other = moved(packed, to_core)
    send_proj = project_call(packed, w_send, atoms, other)
    outer = moved(send_proj, to_outer)
    near = moved(send_proj, to_column)
    beyond = moved(send_proj, to_beyond)
    outer_near = moved(send_proj, lambda s, b: to_outer(*to_column(s, b)))
    outer_beyond = moved(send_proj, lambda s, b: to_outer(*to_beyond(s, b)))

    plane, line = plane_groups(slabs, subs), line_groups(slabs, subs)
    slab = lax.axis_index("slab")
    mine = (slab % 2) * (len(plane[0]) // 2) + lax.axis_index("sub") * (PLANE // 2)
    mine = mine + slab % PLANE // 2
    sums = factor_call(packed, other, atoms)
    core = moved(column_call((send_proj, near, beyond), outer_beyond), to_core)
    blocks = [send_proj, near, beyond, core, outer, outer_near, outer_beyond]
    cores = core_groups(slabs, subs)
    stage_one = stage_call(exchanged(sums, cores), len(cores[0]), len(line[0]))
    count = stage_one.shape[1]
    weights = wave_weights(kgrid, k_filter, mine * count, count)
    norm_factor = 1.0 / math.sqrt(atoms * DEVICES)
    filtered = filter_call(
        exchanged(stage_one, line), weights, w_mix, norm_factor, len(plane[0])
    )
    factors = exchanged(filtered, plane).reshape(DEVICES, -1)

    after = [stage_one, filtered]
    parts = [
        edge_call(p, after[p], senders, edge_basis, features, w_recv, w_basis, w_out, blocks)
        for p in range(len(PARTS))
    ]
    return final_call(atom_count, positions, factors, parts, 4.0 / math.sqrt(total_k))


def solution(mesh):
    placed = (
        P(("slab", "sub"), None),
        P(None, ("slab", "sub")),
        P(("slab", "sub")),
        P(), P(), P(), P(), P(), P(), P(),
        P(None, ("slab", "sub")),
        P(("slab", "sub")),
    )
    return jax.shard_map(
        per_device, mesh=mesh, in_specs=placed, out_specs=P(("slab", "sub"), None), check_vma=False
    )
```

```python
import functools
import math

import jax
import jax.numpy as jnp
import numpy as np
from jax import lax
from jax.experimental import pallas as pl
from jax.experimental.pallas import tpu as pltpu
from jax.sharding import PartitionSpec as P

TOP = 6
SIDE = 2 * TOP + 1
XY_ROWS = 88
WAVE_ROWS = 2304
DEVICES = 256
ROWS_EACH = WAVE_ROWS // DEVICES
HALF_ROWS = WAVE_ROWS // 2
HALF_TOP = TOP // 2
PARTS = (512, 512)
PLANE = 4
UNROLL = 32
BUFFERS = 2
COS_TERMS = (
    0.999999989059022, -19.7392044994538, 64.93911745989, -85.4501395308031,
    60.1676309503793, -25.9675992464965, 6.52865815867317,
)
SMALL_VMEM, TABLE_VMEM, LARGE_VMEM = 6 * 2**20, 14 * 2**20, 60 * 2**20


def wave_layout():
    flat = [(0, 0)] + [(kx, 0) for kx in range(1, TOP + 1)]
    flat += [(kx, ky) for ky in range(1, TOP + 1) for kx in range(-TOP, TOP + 1)]
    codes = np.full((2, HALF_ROWS), -1, np.int32)
    xy = np.zeros((XY_ROWS, 2), np.float32)

    def code(kx, ky, kz):
        return ((kz + TOP) * SIDE + ky + TOP) * SIDE + kx + TOP

    for row, (kx, ky) in enumerate(flat):
        xy[row] = kx, ky
        for kz in range(1, TOP + 1):
            half, at = divmod(kz - 1, HALF_TOP)
            base = at * 4 * XY_ROWS + row
            codes[half, base] = code(kx, ky, kz)
            codes[half, base + 2 * XY_ROWS] = code(kx, ky, kz)
            if row > 0:
                codes[half, base + XY_ROWS] = code(-kx, -ky, kz)
                codes[half, base + 3 * XY_ROWS] = code(-kx, -ky, kz)
        base = HALF_TOP * 4 * XY_ROWS + row
        codes[0, base] = code(kx, ky, 0)
        if row > 0:
            codes[1, base] = code(kx, ky, 0)
    each = DEVICES // 2
    codes = codes.reshape(2, ROWS_EACH, each).transpose(1, 0, 2)
    return xy, codes.reshape(ROWS_EACH, DEVICES)


XY, CODES = wave_layout()


def turn_waves(turns):
    rest = turns - jnp.floor(turns + 0.5)
    quarter = rest - 0.25
    quarter = jnp.where(quarter < -0.5, quarter + 1.0, quarter)

    def cosine(part):
        square = part * part
        total = jnp.full_like(square, COS_TERMS[-1])
        for term in COS_TERMS[-2::-1]:
            total = total * square + term
        return total

    return cosine(rest), cosine(quarter)


def flat_waves(xy_ref, pos_ref, first, width):
    wide = (XY_ROWS, width)
    coords = [jnp.broadcast_to(pos_ref[d : d + 1, first : first + width], wide) for d in range(2)]
    flat_turns = (
        jnp.broadcast_to(xy_ref[:, 0:1], wide) * coords[0]
        + jnp.broadcast_to(xy_ref[:, 1:2], wide) * coords[1]
    )
    return turn_waves(flat_turns)


def half_table(flat, pos_ref, first, half):
    cos_xy, sin_xy = flat
    wide = cos_xy.shape
    width = wide[1]
    steps = lax.broadcasted_iota(jnp.int32, (8, width), 0) + (1 + HALF_TOP * half)
    cos_z, sin_z = turn_waves(
        steps.astype(jnp.float32)
        * jnp.broadcast_to(pos_ref[2:3, first : first + width], (8, width))
    )
    rows = []
    for at in range(HALF_TOP):
        cos_k = jnp.broadcast_to(cos_z[at : at + 1], wide)
        sin_k = jnp.broadcast_to(sin_z[at : at + 1], wide)
        both_cos, both_sin = cos_xy * cos_k, sin_xy * sin_k
        sin_cos, cos_sin = sin_xy * cos_k, cos_xy * sin_k
        rows += [both_cos - both_sin, both_cos + both_sin, cos_sin + sin_cos, cos_sin - sin_cos]
    rows.append(jnp.where(half == 0, cos_xy, sin_xy))
    rows.append(jnp.zeros((HALF_ROWS - (4 * HALF_TOP + 1) * XY_ROWS, width), jnp.float32))
    return jnp.concatenate(rows, axis=0).astype(jnp.bfloat16)


def hbm():
    return pl.BlockSpec(memory_space=pltpu.HBM)


def vmem():
    return pl.BlockSpec(memory_space=pltpu.VMEM)


def limit(size):
    return pltpu.CompilerParams(vmem_limit_bytes=size)


def loads(sources, targets, arrivals):
    copies = [
        pltpu.make_async_copy(source, target, arrivals.at[at])
        for at, (source, target) in enumerate(zip(sources, targets))
    ]
    for copy in copies:
        copy.start()
    return copies


def packed_rows(atoms):
    return 3 * 8 * atoms // 128


def prepare_kernel(count_ref, pos_hbm, features_hbm, packed_ref, *refs):
    pos_ref, features_ref, wide_ref, arrivals = refs
    copies = loads((pos_hbm, features_hbm), (pos_ref, features_ref), arrivals)
    atoms, channels = features_ref.shape
    wide_ref[...] = jnp.zeros_like(wide_ref)
    for copy in copies:
        copy.wait()
    live = lax.broadcasted_iota(jnp.int32, (atoms, channels), 0) < count_ref[0]
    masked = jnp.where(live, features_ref[...].astype(jnp.float32), 0.0).astype(jnp.bfloat16)
    packed_ref[0:atoms, :] = masked
    wide_ref[0:3, :] = pos_ref[...]
    rest = wide_ref[...]
    pieces = []
    for _ in range(3):
        piece = rest.astype(jnp.bfloat16).astype(jnp.float32)
        rest = rest - piece
        pieces += [piece[:, at : at + 128] for at in range(0, atoms, 128)]
    packed_ref[atoms:, :] = jnp.concatenate(pieces, axis=0).astype(jnp.bfloat16)


def prepare_call(atom_count, positions, features):
    atoms, channels = features.shape
    return pl.pallas_call(
        prepare_kernel,
        in_specs=[pl.BlockSpec(memory_space=pltpu.SMEM), hbm(), hbm()],
        out_specs=vmem(),
        out_shape=jax.ShapeDtypeStruct((atoms + packed_rows(atoms), channels), jnp.bfloat16),
        scratch_shapes=[
            pltpu.VMEM(positions.shape, jnp.float32),
            pltpu.VMEM(features.shape, jnp.bfloat16),
            pltpu.VMEM((8, atoms), jnp.float32),
            pltpu.SemaphoreType.DMA((2,)),
        ],
        compiler_params=limit(SMALL_VMEM),
        name="prepare_rows",
    )(atom_count, positions, features)


def project_kernel(packed_ref, send_ref, after_ref, out_ref):
    del after_ref
    rows = packed_ref[0 : out_ref.shape[0], :]
    out_ref[...] = jnp.dot(rows, send_ref[...], preferred_element_type=jnp.float32).astype(
        jnp.bfloat16
    )


def project_call(packed, w_send, atoms, after):
    return pl.pallas_call(
        project_kernel,
        in_specs=[vmem(), vmem(), pl.BlockSpec(memory_space=pl.ANY)],
        out_specs=vmem(),
        out_shape=jax.ShapeDtypeStruct((atoms, w_send.shape[1]), jnp.bfloat16),
        compiler_params=limit(SMALL_VMEM),
        name="project_rows",
    )(packed, w_send, after)


def factor_kernel(xy_hbm, packed_any, other_any, *refs):
    sums_ref, table_ref, xy_ref, packed_ref, pos_ref, arrivals = refs
    copies = loads(
        (xy_hbm, packed_any, other_any), (xy_ref, packed_ref.at[0], packed_ref.at[1]), arrivals
    )
    half = lax.rem(lax.axis_index("slab"), 2)
    atoms = pos_ref.shape[1]
    channels = packed_ref.shape[2]
    for copy in copies:
        copy.wait()
    tiles = atoms // 128
    for side in range(2):
        values = packed_ref[side, atoms:, :].astype(jnp.float32)
        for at in range(tiles):
            total = None
            for piece in range(3):
                start = (piece * tiles + at) * 8
                part = values[start : start + 8]
                total = part if total is None else total + part
            pos_ref[:, at * 128 : (at + 1) * 128] = total
        for first in range(0, atoms, 128):
            table_ref[:, side * atoms + first : side * atoms + first + 128] = half_table(
                flat_waves(xy_ref, pos_ref, first, 128), pos_ref, first, half
            )
    each = sums_ref.shape[0]
    for r in range(ROWS_EACH):
        rows = table_ref[r * each : (r + 1) * each, :]
        sums_ref[:, r * channels : (r + 1) * channels] = jnp.dot(
            rows[:, :atoms], packed_ref[0, :atoms, :], preferred_element_type=jnp.float32
        ) + jnp.dot(
            rows[:, atoms:], packed_ref[1, :atoms, :], preferred_element_type=jnp.float32
        )


def factor_call(packed, other, atoms):
    channels = packed.shape[1]
    anywhere = pl.BlockSpec(memory_space=pl.ANY)
    return pl.pallas_call(
        factor_kernel,
        in_specs=[hbm(), anywhere, anywhere],
        out_specs=vmem(),
        out_shape=jax.ShapeDtypeStruct((DEVICES // 2, ROWS_EACH * channels), jnp.float32),
        scratch_shapes=[
            pltpu.VMEM((HALF_ROWS, 2 * atoms), jnp.bfloat16),
            pltpu.VMEM(XY.shape, jnp.float32),
            pltpu.VMEM((2,) + packed.shape, jnp.bfloat16),
            pltpu.VMEM((8, atoms), jnp.float32),
            pltpu.SemaphoreType.DMA((3,)),
        ],
        compiler_params=limit(TABLE_VMEM),
        name="factor_sums",
    )(jnp.asarray(XY), packed, other)


def stage_kernel(sums_ref, out_ref):
    rows = out_ref.shape[1]
    total = sums_ref[0:rows, :]
    for at in range(rows, sums_ref.shape[0], rows):
        total = total + sums_ref[at : at + rows, :]
    for at in range(out_ref.shape[0]):
        out_ref[at] = total


def stage_call(sums, sources, copies):
    return pl.pallas_call(
        stage_kernel,
        out_specs=vmem(),
        out_shape=jax.ShapeDtypeStruct(
            (copies, sums.shape[0] // sources, sums.shape[1]), jnp.float32
        ),
        compiler_params=limit(SMALL_VMEM),
        name="stage_sums",
    )(sums)


def filter_kernel(norm_factor, sums_ref, weight_ref, mix_hbm, out_ref, mix_ref, arrivals):
    copies = loads((mix_hbm,), (mix_ref,), arrivals)
    channels = mix_ref.shape[0]
    total = sums_ref[0]
    for at in range(1, sums_ref.shape[0]):
        total = total + sums_ref[at]
    count = total.shape[0]
    scaled = jnp.concatenate(
        [total[:, r * channels : (r + 1) * channels] for r in range(ROWS_EACH)], axis=0
    )
    scaled = scaled * norm_factor * weight_ref[...]
    copies[0].wait()
    mixed = jnp.dot(
        scaled, mix_ref[...], precision=lax.Precision.HIGHEST, preferred_element_type=jnp.float32
    )
    lines = jnp.concatenate(
        [mixed[r * count : (r + 1) * count] for r in range(ROWS_EACH)], axis=1
    ).astype(jnp.bfloat16)
    for at in range(out_ref.shape[0]):
        out_ref[at] = lines


def filter_call(sums, weights, w_mix, norm_factor, copies):
    return pl.pallas_call(
        functools.partial(filter_kernel, norm_factor),
        in_specs=[vmem(), vmem(), hbm()],
        out_specs=vmem(),
        out_shape=jax.ShapeDtypeStruct((copies,) + sums.shape[1:], jnp.bfloat16),
        scratch_shapes=[pltpu.VMEM(w_mix.shape, jnp.float32), pltpu.SemaphoreType.DMA((1,))],
        compiler_params=limit(SMALL_VMEM),
        name="filter_rows",
    )(sums, weights, w_mix)


def wave_weights(kgrid, k_filter, first, count):
    kx, ky, kz = kgrid[0], kgrid[1], kgrid[2]
    low = (kz < 0) | ((kz == 0) & ((ky < 0) | ((ky == 0) & (kx < 0))))
    sign = jnp.where(low, -1, 1)
    code = ((kz * sign + TOP) * SIDE + ky * sign + TOP) * SIDE + kx * sign + TOP
    mine = lax.dynamic_slice_in_dim(jnp.asarray(CODES), first, count, 1).reshape(-1)
    same = (mine[:, None] == code[None, :]).astype(jnp.float32)
    return jnp.dot(same, k_filter, precision=lax.Precision.HIGHEST)


def edge_kernel(
    degree, first, ids_hbm, basis_hbm, features_hbm, recv_hbm, wb_hbm, wo_hbm, *refs
):
    blocks, refs = refs[:7], refs[7:]
    (after_ref, out_ref, pool_ref, radial_ref, part_ref, own_ref, wide_ref), refs = refs[:7], refs[7:]
    local, held, loaded, landed, refs = refs[:6], refs[6:13], refs[13], refs[14], refs[15:]
    ids_ref, basis_ref, features_ref, recv_ref, wb_ref, wo_ref = local
    buffers, arrivals = refs[:BUFFERS], refs[BUFFERS:]
    atoms, channels = out_ref.shape
    del after_ref
    copies = loads(
        (
            ids_hbm.at[pl.ds(first * degree // 128, atoms * degree // 128), :],
            basis_hbm.at[:, pl.ds(first * degree, atoms * degree)],
            features_hbm.at[pl.ds(first, atoms), :],
            recv_hbm,
            wb_hbm,
            wo_hbm,
        ),
        local,
        loaded,
    )
    landing = loads(blocks, held, landed)
    edges = UNROLL * degree
    lines = edges // 128
    chunks = atoms // UNROLL

    def fetch(chunk, at):
        source = ids_ref.at[pl.ds(chunk * lines, lines), :]
        return pltpu.make_async_copy(source, buffers[at], arrivals[at])

    slab_even = lax.rem(lax.axis_index("slab"), 2) == 0
    sub_even = lax.rem(lax.axis_index("sub"), 2) == 0
    slab_place = (1, jnp.where(slab_even, 2, 0), jnp.where(slab_even, 0, 2))
    sub_place = (1, jnp.where(sub_even, 2, 0), jnp.where(sub_even, 0, 2))
    for copy in copies:
        copy.wait()
    for at in range(BUFFERS):
        fetch(at, at).start()
    own_ref[...] = jnp.dot(features_ref[...], recv_ref[...], preferred_element_type=jnp.float32)

    basis_rows = wb_ref.shape[0]
    groups = 128 // basis_rows
    stacked = jnp.concatenate([wb_ref[...].astype(jnp.float32)] * groups, axis=0)
    group_of = lax.broadcasted_iota(jnp.int32, stacked.shape, 0) // basis_rows
    for g in range(groups):
        wide_ref[:, g * channels : (g + 1) * channels] = jnp.where(
            group_of == g, stacked, 0.0
        ).astype(jnp.bfloat16)

    span = groups * 128

    def radial_block(step, carry):
        turned = []
        for at in range(4):
            values = basis_ref[:, pl.ds(pl.multiple_of((step * 4 + at) * span, span), span)]
            values = values.astype(jnp.float32)
            stack = jnp.concatenate(
                [values[:, g * 128 : (g + 1) * 128] for g in range(groups)], axis=0
            )
            turned.append(stack.T.astype(jnp.bfloat16))
        turned = jnp.concatenate(turned, axis=0)
        for g in range(0, groups, 2):
            both = jnp.dot(
                turned,
                wide_ref[:, g * channels : (g + 2) * channels],
                preferred_element_type=jnp.float32,
            )
            for at in range(4):
                base = pl.multiple_of((step * 4 + at) * span, span) + g * 128
                half = both[at * 128 : (at + 1) * 128]
                radial_ref[pl.ds(base, 128), :] = half[:, :channels]
                radial_ref[pl.ds(base + 128, 128), :] = half[:, channels:]
        return carry

    lax.fori_loop(0, atoms * degree // span // 4, radial_block, 0)
    rows = blocks[0].shape[0]
    at = 0
    for copy, block in zip(landing, held):
        copy.wait()
        for first_row in range(0, block.shape[0], rows):
            place = pl.multiple_of((slab_place[at // 3] * 3 + sub_place[at % 3]) * rows, rows)
            pool_ref[pl.ds(place, rows), :] = block[first_row : first_row + rows, :].astype(
                jnp.float32
            )
            at += 1

    sublane = lax.broadcasted_iota(jnp.int32, (8, channels), 0)
    at_sublane = [sublane == r for r in range(8)]

    def some_atoms(chunk, ids):
        own = own_ref.at[pl.ds(pl.multiple_of(chunk * UNROLL, UNROLL), UNROLL), :]
        part = part_ref.at[pl.ds(pl.multiple_of(chunk * UNROLL * 8, UNROLL * 8), UNROLL * 8), :]
        radial = radial_ref.at[pl.ds(pl.multiple_of(chunk * edges, edges), edges), :]
        for u in range(UNROLL):
            mine = jnp.broadcast_to(own[u : u + 1, :], (8, channels))
            total = None
            for edge in range(u * degree, (u + 1) * degree, 8):
                sent = None
                for r in range(8):
                    sender = ids[(edge + r) // 128, (edge + r) % 128]
                    row = jnp.broadcast_to(pool_ref[pl.ds(sender, 1), :], (8, channels))
                    sent = row if sent is None else jnp.where(at_sublane[r], row, sent)
                half = (sent + radial[edge : edge + 8, :] + mine) * 0.5
                hidden = (half + half * jnp.tanh(half)).astype(jnp.bfloat16).astype(jnp.float32)
                total = hidden if total is None else total + hidden
            part[u * 8 : u * 8 + 8, :] = total

    def round_of_chunks(step, carry):
        for at in range(BUFFERS):
            chunk = step * BUFFERS + at
            fetch(chunk, at).wait()
            some_atoms(chunk, buffers[at])
            fetch(jnp.minimum(chunk + BUFFERS, chunks - 1), at).start()
        return carry

    lax.fori_loop(0, chunks // BUFFERS, round_of_chunks, 0)
    for at in range(BUFFERS):
        fetch(chunks - 1, at).wait()
    summed = part_ref[pl.ds(0, atoms, stride=8), :]
    for r in range(1, 8):
        summed = summed + part_ref[pl.ds(r, atoms, stride=8), :]
    high = summed.astype(jnp.bfloat16)
    low = (summed - high.astype(jnp.float32)).astype(jnp.bfloat16)
    message = jnp.dot(high, wo_ref[...], preferred_element_type=jnp.float32) + jnp.dot(
        low, wo_ref[...], preferred_element_type=jnp.float32
    )
    out_ref[...] = message * (1.0 / math.sqrt(degree))


def edge_call(part, after, senders, edge_basis, features, w_recv, w_basis, w_out, blocks):
    channels = features.shape[1]
    degree = senders.shape[0] // features.shape[0]
    atoms, first = PARTS[part], sum(PARTS[:part])
    rows = sum(block.shape[0] for block in blocks)
    return pl.pallas_call(
        functools.partial(edge_kernel, degree, first),
        in_specs=[hbm()] * 6 + [pl.BlockSpec(memory_space=pl.ANY)] * (len(blocks) + 1),
        out_specs=vmem(),
        out_shape=jax.ShapeDtypeStruct((atoms, channels), jnp.float32),
        scratch_shapes=[
            pltpu.VMEM((rows, channels), jnp.float32),
            pltpu.VMEM((atoms * degree, channels), jnp.float32),
            pltpu.VMEM((atoms * 8, channels), jnp.float32),
            pltpu.VMEM((atoms, channels), jnp.float32),
            pltpu.VMEM((128, 128 // w_basis.shape[0] * channels), jnp.bfloat16),
            pltpu.VMEM((atoms * degree // 128, 128), jnp.int32),
            pltpu.VMEM((edge_basis.shape[0], atoms * degree), jnp.bfloat16),
            pltpu.VMEM((atoms, channels), jnp.bfloat16),
            pltpu.VMEM(w_recv.shape, jnp.bfloat16),
            pltpu.VMEM(w_basis.shape, jnp.bfloat16),
            pltpu.VMEM(w_out.shape, jnp.bfloat16),
        ]
        + [pltpu.VMEM(block.shape, jnp.bfloat16) for block in blocks]
        + [pltpu.SemaphoreType.DMA((6,)), pltpu.SemaphoreType.DMA((len(blocks),))]
        + [pltpu.SMEM((UNROLL * degree // 128, 128), jnp.int32)] * BUFFERS
        + [pltpu.SemaphoreType.DMA] * BUFFERS,
        compiler_params=limit(LARGE_VMEM),
        cost_estimate=pl.CostEstimate(
            flops=8 * 10**9, bytes_accessed=4 * 10**6, transcendentals=10**6
        ),
        name="edge_part_%d" % part,
    )(
        senders.reshape(-1, 128), edge_basis, features, w_recv, w_basis, w_out, *blocks, after
    )


def final_kernel(scale, count_ref, xy_hbm, pos_hbm, factors_ref, *refs):
    parts, (out_ref, xy_ref, pos_ref, arrivals) = refs[:-4], refs[-4:]
    copies = loads((xy_hbm, pos_hbm), (xy_ref, pos_ref), arrivals)
    channels = out_ref.shape[1]
    each = DEVICES // 2
    factors = jnp.concatenate(
        [
            factors_ref[half * each : (half + 1) * each, r * channels : (r + 1) * channels]
            for half in range(2)
            for r in range(ROWS_EACH)
        ],
        axis=0,
    ).T
    total, first = out_ref.shape[0], 0
    for part in parts:
        out_ref[first : first + part.shape[0], :] = part[...]
        first += part.shape[0]
    for copy in copies:
        copy.wait()
    atoms = 256
    for first in range(0, total, atoms):
        flat = flat_waves(xy_ref, pos_ref, first, atoms)
        table = jnp.concatenate(
            [half_table(flat, pos_ref, first, half) for half in range(2)], axis=0
        )
        field = jnp.dot(factors, table, preferred_element_type=jnp.float32)
        live = first + lax.broadcasted_iota(jnp.int32, (atoms, channels), 0) < count_ref[0]
        near = out_ref[first : first + atoms, :]
        out_ref[first : first + atoms, :] = jnp.where(live, near + field.T * scale, 0.0)


def final_call(atom_count, positions, factors, parts, scale):
    atoms = sum(part.shape[0] for part in parts)
    channels = parts[0].shape[1]
    return pl.pallas_call(
        functools.partial(final_kernel, scale),
        in_specs=[pl.BlockSpec(memory_space=pltpu.SMEM), hbm(), hbm(), vmem()]
        + [vmem()] * len(parts),
        out_specs=vmem(),
        out_shape=jax.ShapeDtypeStruct((atoms, channels), jnp.float32),
        scratch_shapes=[
            pltpu.VMEM(XY.shape, jnp.float32),
            pltpu.VMEM(positions.shape, jnp.float32),
            pltpu.SemaphoreType.DMA((2,)),
        ],
        compiler_params=limit(TABLE_VMEM),
        name="updated_rows",
    )(atom_count, jnp.asarray(XY), positions, factors, *parts)


def column_kernel(own_ref, near_ref, beyond_ref, after_ref, out_ref):
    del after_ref
    rows = own_ref.shape[0]
    for at, block in enumerate((own_ref, near_ref, beyond_ref)):
        out_ref[at * rows : (at + 1) * rows, :] = block[...]


def column_call(blocks, after):
    rows, channels = blocks[0].shape
    return pl.pallas_call(
        column_kernel,
        in_specs=[vmem()] * 3 + [pl.BlockSpec(memory_space=pl.ANY)],
        out_specs=vmem(),
        out_shape=jax.ShapeDtypeStruct((3 * rows, channels), blocks[0].dtype),
        compiler_params=limit(SMALL_VMEM),
        name="column_rows",
    )(*blocks, after)


def moved(array, target):
    slabs, subs = lax.axis_size("slab"), lax.axis_size("sub")
    pairs = []
    for s in range(slabs):
        for b in range(subs):
            to_s, to_b = target(s, b)
            pairs.append((s * subs + b, to_s % slabs * subs + to_b % subs))
    return lax.ppermute(array, ("slab", "sub"), pairs)


def to_core(s, b):
    return s ^ 1, b


def to_outer(s, b):
    return s + (1 if s % 2 else -1), b


def to_column(s, b):
    return s, b ^ 1


def to_beyond(s, b):
    return s, b + (-1 if b % 2 == 0 else 1)


def plane_groups(slabs, subs):
    return [
        [
            (z * PLANE + 2 * q + core) * subs + b
            for core in range(2)
            for b in range(subs)
            for q in range(PLANE // 2)
        ]
        for z in range(slabs // PLANE)
    ]


def core_groups(slabs, subs):
    planes = plane_groups(slabs, subs)
    half = len(planes[0]) // 2
    return [group[core * half : (core + 1) * half] for group in planes for core in range(2)]


def line_groups(slabs, subs):
    return [
        [(z * PLANE + q) * subs + b for z in range(slabs // PLANE)]
        for b in range(subs)
        for q in range(PLANE)
    ]


def exchanged(array, groups):
    return lax.all_to_all(array, ("slab", "sub"), 0, 0, axis_index_groups=groups, tiled=True)


def per_device(
    features, positions, atom_count, kgrid, k_filter, w_mix, w_recv, w_send, w_basis, w_out,
    edge_basis, senders,
):
    atoms, channels = features.shape
    total_k = kgrid.shape[1]
    subs, slabs = lax.axis_size("sub"), lax.axis_size("slab")
    packed = prepare_call(atom_count, positions, features)
    other = moved(packed, to_core)
    send_proj = project_call(packed, w_send, atoms, other)
    outer = moved(send_proj, to_outer)
    near = moved(send_proj, to_column)
    beyond = moved(send_proj, to_beyond)
    outer_near = moved(send_proj, lambda s, b: to_outer(*to_column(s, b)))
    outer_beyond = moved(send_proj, lambda s, b: to_outer(*to_beyond(s, b)))

    plane, line = plane_groups(slabs, subs), line_groups(slabs, subs)
    slab = lax.axis_index("slab")
    mine = (slab % 2) * (len(plane[0]) // 2) + lax.axis_index("sub") * (PLANE // 2)
    mine = mine + slab % PLANE // 2
    sums = factor_call(packed, other, atoms)
    core = moved(column_call((send_proj, near, beyond), outer_beyond), to_core)
    blocks = [send_proj, near, beyond, core, outer, outer_near, outer_beyond]
    cores = core_groups(slabs, subs)
    stage_one = stage_call(exchanged(sums, cores), len(cores[0]), len(line[0]))
    count = stage_one.shape[1]
    weights = wave_weights(kgrid, k_filter, mine * count, count)
    norm_factor = 1.0 / math.sqrt(atoms * DEVICES)
    filtered = filter_call(
        exchanged(stage_one, line), weights, w_mix, norm_factor, len(plane[0])
    )
    factors = exchanged(filtered, plane).reshape(DEVICES, -1)

    after = [stage_one, filtered]
    parts = [
        edge_call(p, after[p], senders, edge_basis, features, w_recv, w_basis, w_out, blocks)
        for p in range(len(PARTS))
    ]
    return final_call(atom_count, positions, factors, parts, 4.0 / math.sqrt(total_k))


def solution(mesh):
    placed = (
        P(("slab", "sub"), None),
        P(None, ("slab", "sub")),
        P(("slab", "sub")),
        P(), P(), P(), P(), P(), P(), P(),
        P(None, ("slab", "sub")),
        P(("slab", "sub")),
    )
    return jax.shard_map(
        per_device, mesh=mesh, in_specs=placed, out_specs=P(("slab", "sub"), None), check_vma=False
    )
```

```python
import functools
import math

import jax
import jax.numpy as jnp
import numpy as np
from jax import lax
from jax.experimental import pallas as pl
from jax.experimental.pallas import tpu as pltpu
from jax.sharding import PartitionSpec as P

TOP = 6
SIDE = 2 * TOP + 1
XY_ROWS = 88
WAVE_ROWS = 2304
DEVICES = 256
ROWS_EACH = WAVE_ROWS // DEVICES
HALF_ROWS = WAVE_ROWS // 2
HALF_TOP = TOP // 2
PARTS = (512, 512)
PLANE = 4
UNROLL = 32
BUFFERS = 2
COS_TERMS = (
    0.999999989059022, -19.7392044994538, 64.93911745989, -85.4501395308031,
    60.1676309503793, -25.9675992464965, 6.52865815867317,
)
SMALL_VMEM, TABLE_VMEM, LARGE_VMEM = 6 * 2**20, 14 * 2**20, 60 * 2**20


def wave_layout():
    flat = [(0, 0)] + [(kx, 0) for kx in range(1, TOP + 1)]
    flat += [(kx, ky) for ky in range(1, TOP + 1) for kx in range(-TOP, TOP + 1)]
    codes = np.full((2, HALF_ROWS), -1, np.int32)
    xy = np.zeros((XY_ROWS, 2), np.float32)

    def code(kx, ky, kz):
        return ((kz + TOP) * SIDE + ky + TOP) * SIDE + kx + TOP

    for row, (kx, ky) in enumerate(flat):
        xy[row] = kx, ky
        for kz in range(1, TOP + 1):
            half, at = divmod(kz - 1, HALF_TOP)
            base = at * 4 * XY_ROWS + row
            codes[half, base] = code(kx, ky, kz)
            codes[half, base + 2 * XY_ROWS] = code(kx, ky, kz)
            if row > 0:
                codes[half, base + XY_ROWS] = code(-kx, -ky, kz)
                codes[half, base + 3 * XY_ROWS] = code(-kx, -ky, kz)
        base = HALF_TOP * 4 * XY_ROWS + row
        codes[0, base] = code(kx, ky, 0)
        if row > 0:
            codes[1, base] = code(kx, ky, 0)
    each = DEVICES // 2
    codes = codes.reshape(2, ROWS_EACH, each).transpose(1, 0, 2)
    return xy, codes.reshape(ROWS_EACH, DEVICES)


XY, CODES = wave_layout()


def turn_waves(turns):
    rest = turns - jnp.floor(turns + 0.5)
    quarter = rest - 0.25
    quarter = jnp.where(quarter < -0.5, quarter + 1.0, quarter)

    def cosine(part):
        square = part * part
        total = jnp.full_like(square, COS_TERMS[-1])
        for term in COS_TERMS[-2::-1]:
            total = total * square + term
        return total

    return cosine(rest), cosine(quarter)


def flat_waves(xy_ref, pos_ref, first, width):
    wide = (XY_ROWS, width)
    coords = [jnp.broadcast_to(pos_ref[d : d + 1, first : first + width], wide) for d in range(2)]
    flat_turns = (
        jnp.broadcast_to(xy_ref[:, 0:1], wide) * coords[0]
        + jnp.broadcast_to(xy_ref[:, 1:2], wide) * coords[1]
    )
    return turn_waves(flat_turns)


def half_table(flat, pos_ref, first, half):
    cos_xy, sin_xy = flat
    wide = cos_xy.shape
    width = wide[1]
    steps = lax.broadcasted_iota(jnp.int32, (8, width), 0) + (1 + HALF_TOP * half)
    cos_z, sin_z = turn_waves(
        steps.astype(jnp.float32)
        * jnp.broadcast_to(pos_ref[2:3, first : first + width], (8, width))
    )
    rows = []
    for at in range(HALF_TOP):
        cos_k = jnp.broadcast_to(cos_z[at : at + 1], wide)
        sin_k = jnp.broadcast_to(sin_z[at : at + 1], wide)
        both_cos, both_sin = cos_xy * cos_k, sin_xy * sin_k
        sin_cos, cos_sin = sin_xy * cos_k, cos_xy * sin_k
        rows += [both_cos - both_sin, both_cos + both_sin, cos_sin + sin_cos, cos_sin - sin_cos]
    rows.append(jnp.where(half == 0, cos_xy, sin_xy))
    rows.append(jnp.zeros((HALF_ROWS - (4 * HALF_TOP + 1) * XY_ROWS, width), jnp.float32))
    return jnp.concatenate(rows, axis=0).astype(jnp.bfloat16)


def hbm():
    return pl.BlockSpec(memory_space=pltpu.HBM)


def vmem():
    return pl.BlockSpec(memory_space=pltpu.VMEM)


def limit(size):
    return pltpu.CompilerParams(vmem_limit_bytes=size)


def loads(sources, targets, arrivals):
    copies = [
        pltpu.make_async_copy(source, target, arrivals.at[at])
        for at, (source, target) in enumerate(zip(sources, targets))
    ]
    for copy in copies:
        copy.start()
    return copies


def packed_rows(atoms):
    return 3 * 8 * atoms // 128


def prepare_kernel(count_ref, pos_hbm, features_hbm, packed_ref, *refs):
    pos_ref, features_ref, wide_ref, arrivals = refs
    copies = loads((pos_hbm, features_hbm), (pos_ref, features_ref), arrivals)
    atoms, channels = features_ref.shape
    wide_ref[...] = jnp.zeros_like(wide_ref)
    for copy in copies:
        copy.wait()
    live = lax.broadcasted_iota(jnp.int32, (atoms, channels), 0) < count_ref[0]
    masked = jnp.where(live, features_ref[...].astype(jnp.float32), 0.0).astype(jnp.bfloat16)
    packed_ref[0:atoms, :] = masked
    wide_ref[0:3, :] = pos_ref[...]
    rest = wide_ref[...]
    pieces = []
    for _ in range(3):
        piece = rest.astype(jnp.bfloat16).astype(jnp.float32)
        rest = rest - piece
        pieces += [piece[:, at : at + 128] for at in range(0, atoms, 128)]
    packed_ref[atoms:, :] = jnp.concatenate(pieces, axis=0).astype(jnp.bfloat16)


def prepare_call(atom_count, positions, features):
    atoms, channels = features.shape
    return pl.pallas_call(
        prepare_kernel,
        in_specs=[pl.BlockSpec(memory_space=pltpu.SMEM), hbm(), hbm()],
        out_specs=vmem(),
        out_shape=jax.ShapeDtypeStruct((atoms + packed_rows(atoms), channels), jnp.bfloat16),
        scratch_shapes=[
            pltpu.VMEM(positions.shape, jnp.float32),
            pltpu.VMEM(features.shape, jnp.bfloat16),
            pltpu.VMEM((8, atoms), jnp.float32),
            pltpu.SemaphoreType.DMA((2,)),
        ],
        compiler_params=limit(SMALL_VMEM),
        name="prepare_rows",
    )(atom_count, positions, features)


def project_kernel(packed_ref, send_ref, after_ref, out_ref):
    del after_ref
    rows = packed_ref[0 : out_ref.shape[0], :]
    out_ref[...] = jnp.dot(rows, send_ref[...], preferred_element_type=jnp.float32).astype(
        jnp.bfloat16
    )


def project_call(packed, w_send, atoms, after):
    return pl.pallas_call(
        project_kernel,
        in_specs=[vmem(), vmem(), pl.BlockSpec(memory_space=pl.ANY)],
        out_specs=vmem(),
        out_shape=jax.ShapeDtypeStruct((atoms, w_send.shape[1]), jnp.bfloat16),
        compiler_params=limit(SMALL_VMEM),
        name="project_rows",
    )(packed, w_send, after)


def factor_kernel(xy_hbm, packed_any, other_any, *refs):
    sums_ref, table_ref, xy_ref, packed_ref, pos_ref, arrivals = refs
    copies = loads(
        (xy_hbm, packed_any, other_any), (xy_ref, packed_ref.at[0], packed_ref.at[1]), arrivals
    )
    half = lax.rem(lax.axis_index("slab"), 2)
    atoms = pos_ref.shape[1]
    channels = packed_ref.shape[2]
    for copy in copies:
        copy.wait()
    tiles = atoms // 128
    for side in range(2):
        values = packed_ref[side, atoms:, :].astype(jnp.float32)
        for at in range(tiles):
            total = None
            for piece in range(3):
                start = (piece * tiles + at) * 8
                part = values[start : start + 8]
                total = part if total is None else total + part
            pos_ref[:, at * 128 : (at + 1) * 128] = total
        for first in range(0, atoms, 128):
            table_ref[:, side * atoms + first : side * atoms + first + 128] = half_table(
                flat_waves(xy_ref, pos_ref, first, 128), pos_ref, first, half
            )
    each = sums_ref.shape[0]
    for r in range(ROWS_EACH):
        rows = table_ref[r * each : (r + 1) * each, :]
        sums_ref[:, r * channels : (r + 1) * channels] = jnp.dot(
            rows[:, :atoms], packed_ref[0, :atoms, :], preferred_element_type=jnp.float32
        ) + jnp.dot(
            rows[:, atoms:], packed_ref[1, :atoms, :], preferred_element_type=jnp.float32
        )


def factor_call(packed, other, atoms):
    channels = packed.shape[1]
    anywhere = pl.BlockSpec(memory_space=pl.ANY)
    return pl.pallas_call(
        factor_kernel,
        in_specs=[hbm(), anywhere, anywhere],
        out_specs=vmem(),
        out_shape=jax.ShapeDtypeStruct((DEVICES // 2, ROWS_EACH * channels), jnp.float32),
        scratch_shapes=[
            pltpu.VMEM((HALF_ROWS, 2 * atoms), jnp.bfloat16),
            pltpu.VMEM(XY.shape, jnp.float32),
            pltpu.VMEM((2,) + packed.shape, jnp.bfloat16),
            pltpu.VMEM((8, atoms), jnp.float32),
            pltpu.SemaphoreType.DMA((3,)),
        ],
        compiler_params=limit(TABLE_VMEM),
        name="factor_sums",
    )(jnp.asarray(XY), packed, other)


def stage_kernel(sums_ref, out_ref):
    rows = out_ref.shape[1]
    total = sums_ref[0:rows, :]
    for at in range(rows, sums_ref.shape[0], rows):
        total = total + sums_ref[at : at + rows, :]
    for at in range(out_ref.shape[0]):
        out_ref[at] = total


def stage_call(sums, sources, copies):
    return pl.pallas_call(
        stage_kernel,
        out_specs=vmem(),
        out_shape=jax.ShapeDtypeStruct(
            (copies, sums.shape[0] // sources, sums.shape[1]), jnp.float32
        ),
        compiler_params=limit(SMALL_VMEM),
        name="stage_sums",
    )(sums)


def filter_kernel(norm_factor, sums_ref, weight_ref, mix_hbm, out_ref, mix_ref, arrivals):
    copies = loads((mix_hbm,), (mix_ref,), arrivals)
    channels = mix_ref.shape[0]
    total = sums_ref[0]
    for at in range(1, sums_ref.shape[0]):
        total = total + sums_ref[at]
    count = total.shape[0]
    scaled = jnp.concatenate(
        [total[:, r * channels : (r + 1) * channels] for r in range(ROWS_EACH)], axis=0
    )
    scaled = scaled * norm_factor * weight_ref[...]
    copies[0].wait()
    mixed = jnp.dot(
        scaled, mix_ref[...], precision=lax.Precision.HIGHEST, preferred_element_type=jnp.float32
    )
    lines = jnp.concatenate(
        [mixed[r * count : (r + 1) * count] for r in range(ROWS_EACH)], axis=1
    ).astype(jnp.bfloat16)
    for at in range(out_ref.shape[0]):
        out_ref[at] = lines


def filter_call(sums, weights, w_mix, norm_factor, copies):
    return pl.pallas_call(
        functools.partial(filter_kernel, norm_factor),
        in_specs=[vmem(), vmem(), hbm()],
        out_specs=vmem(),
        out_shape=jax.ShapeDtypeStruct((copies,) + sums.shape[1:], jnp.bfloat16),
        scratch_shapes=[pltpu.VMEM(w_mix.shape, jnp.float32), pltpu.SemaphoreType.DMA((1,))],
        compiler_params=limit(SMALL_VMEM),
        name="filter_rows",
    )(sums, weights, w_mix)


def wave_weights(kgrid, k_filter, first, count):
    kx, ky, kz = kgrid[0], kgrid[1], kgrid[2]
    low = (kz < 0) | ((kz == 0) & ((ky < 0) | ((ky == 0) & (kx < 0))))
    sign = jnp.where(low, -1, 1)
    code = ((kz * sign + TOP) * SIDE + ky * sign + TOP) * SIDE + kx * sign + TOP
    mine = lax.dynamic_slice_in_dim(jnp.asarray(CODES), first, count, 1).reshape(-1)
    same = (mine[:, None] == code[None, :]).astype(jnp.float32)
    return jnp.dot(same, k_filter, precision=lax.Precision.HIGHEST)


def edge_kernel(
    degree, first, count_ref, ids_hbm, basis_hbm, features_hbm, recv_hbm, wb_hbm, wo_hbm, *refs
):
    blocks, refs = refs[:7], refs[7:]
    (after_ref, out_ref, pool_ref, radial_ref, part_ref, own_ref, wide_ref), refs = refs[:7], refs[7:]
    local, held, loaded, landed, refs = refs[:6], refs[6:13], refs[13], refs[14], refs[15:]
    ids_ref, basis_ref, features_ref, recv_ref, wb_ref, wo_ref = local
    buffers, arrivals = refs[:BUFFERS], refs[BUFFERS:]
    atoms, channels = out_ref.shape
    del after_ref
    copies = loads(
        (
            ids_hbm.at[pl.ds(first * degree // 128, atoms * degree // 128), :],
            basis_hbm.at[:, pl.ds(first * degree, atoms * degree)],
            features_hbm.at[pl.ds(first, atoms), :],
            recv_hbm,
            wb_hbm,
            wo_hbm,
        ),
        local,
        loaded,
    )
    landing = loads(blocks, held, landed)
    edges = UNROLL * degree
    lines = edges // 128
    chunks = atoms // UNROLL
    live = jnp.clip(count_ref[0] - first, 0, atoms)

    def fetch(chunk, at):
        source = ids_ref.at[pl.ds(chunk * lines, lines), :]
        return pltpu.make_async_copy(source, buffers[at], arrivals[at])

    slab_even = lax.rem(lax.axis_index("slab"), 2) == 0
    sub_even = lax.rem(lax.axis_index("sub"), 2) == 0
    slab_place = (1, jnp.where(slab_even, 2, 0), jnp.where(slab_even, 0, 2))
    sub_place = (1, jnp.where(sub_even, 2, 0), jnp.where(sub_even, 0, 2))
    for copy in copies:
        copy.wait()
    for at in range(BUFFERS):
        fetch(at, at).start()
    own_ref[...] = jnp.dot(features_ref[...], recv_ref[...], preferred_element_type=jnp.float32)

    basis_rows = wb_ref.shape[0]
    groups = 128 // basis_rows
    stacked = jnp.concatenate([wb_ref[...].astype(jnp.float32)] * groups, axis=0)
    group_of = lax.broadcasted_iota(jnp.int32, stacked.shape, 0) // basis_rows
    for g in range(groups):
        wide_ref[:, g * channels : (g + 1) * channels] = jnp.where(
            group_of == g, stacked, 0.0
        ).astype(jnp.bfloat16)

    span = groups * 128

    def radial_block(step, carry):
        turned = []
        for at in range(4):
            values = basis_ref[:, pl.ds(pl.multiple_of((step * 4 + at) * span, span), span)]
            values = values.astype(jnp.float32)
            stack = jnp.concatenate(
                [values[:, g * 128 : (g + 1) * 128] for g in range(groups)], axis=0
            )
            turned.append(stack.T.astype(jnp.bfloat16))
        turned = jnp.concatenate(turned, axis=0)
        for g in range(0, groups, 2):
            both = jnp.dot(
                turned,
                wide_ref[:, g * channels : (g + 2) * channels],
                preferred_element_type=jnp.float32,
            )
            for at in range(4):
                base = pl.multiple_of((step * 4 + at) * span, span) + g * 128
                half = both[at * 128 : (at + 1) * 128]
                radial_ref[pl.ds(base, 128), :] = half[:, :channels]
                radial_ref[pl.ds(base + 128, 128), :] = half[:, channels:]
        return carry

    step_atoms = 4 * span // degree
    lax.fori_loop(0, lax.div(live + (step_atoms - 1), step_atoms), radial_block, 0)
    rows = blocks[0].shape[0]
    at = 0
    for copy, block in zip(landing, held):
        copy.wait()
        for first_row in range(0, block.shape[0], rows):
            place = pl.multiple_of((slab_place[at // 3] * 3 + sub_place[at % 3]) * rows, rows)
            pool_ref[pl.ds(place, rows), :] = block[first_row : first_row + rows, :].astype(
                jnp.float32
            )
            at += 1

    sublane = lax.broadcasted_iota(jnp.int32, (8, channels), 0)
    at_sublane = [sublane == r for r in range(8)]

    def some_atoms(chunk, ids):
        own = own_ref.at[pl.ds(pl.multiple_of(chunk * UNROLL, UNROLL), UNROLL), :]
        part = part_ref.at[pl.ds(pl.multiple_of(chunk * UNROLL * 8, UNROLL * 8), UNROLL * 8), :]
        radial = radial_ref.at[pl.ds(pl.multiple_of(chunk * edges, edges), edges), :]
        for u in range(UNROLL):
            mine = jnp.broadcast_to(own[u : u + 1, :], (8, channels))
            total = None
            for edge in range(u * degree, (u + 1) * degree, 8):
                sent = None
                for r in range(8):
                    sender = ids[(edge + r) // 128, (edge + r) % 128]
                    row = jnp.broadcast_to(pool_ref[pl.ds(sender, 1), :], (8, channels))
                    sent = row if sent is None else jnp.where(at_sublane[r], row, sent)
                half = (sent + radial[edge : edge + 8, :] + mine) * 0.5
                hidden = (half + half * jnp.tanh(half)).astype(jnp.bfloat16).astype(jnp.float32)
                total = hidden if total is None else total + hidden
            part[u * 8 : u * 8 + 8, :] = total

    def round_of_chunks(step, carry):
        for at in range(BUFFERS):
            chunk = step * BUFFERS + at
            fetch(chunk, at).wait()
            some_atoms(chunk, buffers[at])
            fetch(jnp.minimum(chunk + BUFFERS, chunks - 1), at).start()
        return carry

    round_atoms = UNROLL * BUFFERS
    lax.fori_loop(0, lax.div(live + (round_atoms - 1), round_atoms), round_of_chunks, 0)
    for at in range(BUFFERS):
        fetch(chunks - 1, at).wait()
    summed = part_ref[pl.ds(0, atoms, stride=8), :]
    for r in range(1, 8):
        summed = summed + part_ref[pl.ds(r, atoms, stride=8), :]
    high = summed.astype(jnp.bfloat16)
    low = (summed - high.astype(jnp.float32)).astype(jnp.bfloat16)
    message = jnp.dot(high, wo_ref[...], preferred_element_type=jnp.float32) + jnp.dot(
        low, wo_ref[...], preferred_element_type=jnp.float32
    )
    out_ref[...] = message * (1.0 / math.sqrt(degree))


def edge_call(part, after, atom_count, senders, edge_basis, features, w_recv, w_basis, w_out, blocks):
    channels = features.shape[1]
    degree = senders.shape[0] // features.shape[0]
    atoms, first = PARTS[part], sum(PARTS[:part])
    rows = sum(block.shape[0] for block in blocks)
    return pl.pallas_call(
        functools.partial(edge_kernel, degree, first),
        in_specs=[pl.BlockSpec(memory_space=pltpu.SMEM)]
        + [hbm()] * 6
        + [pl.BlockSpec(memory_space=pl.ANY)] * (len(blocks) + 1),
        out_specs=vmem(),
        out_shape=jax.ShapeDtypeStruct((atoms, channels), jnp.float32),
        scratch_shapes=[
            pltpu.VMEM((rows, channels), jnp.float32),
            pltpu.VMEM((atoms * degree, channels), jnp.float32),
            pltpu.VMEM((atoms * 8, channels), jnp.float32),
            pltpu.VMEM((atoms, channels), jnp.float32),
            pltpu.VMEM((128, 128 // w_basis.shape[0] * channels), jnp.bfloat16),
            pltpu.VMEM((atoms * degree // 128, 128), jnp.int32),
            pltpu.VMEM((edge_basis.shape[0], atoms * degree), jnp.bfloat16),
            pltpu.VMEM((atoms, channels), jnp.bfloat16),
            pltpu.VMEM(w_recv.shape, jnp.bfloat16),
            pltpu.VMEM(w_basis.shape, jnp.bfloat16),
            pltpu.VMEM(w_out.shape, jnp.bfloat16),
        ]
        + [pltpu.VMEM(block.shape, jnp.bfloat16) for block in blocks]
        + [pltpu.SemaphoreType.DMA((6,)), pltpu.SemaphoreType.DMA((len(blocks),))]
        + [pltpu.SMEM((UNROLL * degree // 128, 128), jnp.int32)] * BUFFERS
        + [pltpu.SemaphoreType.DMA] * BUFFERS,
        compiler_params=limit(LARGE_VMEM),
        cost_estimate=pl.CostEstimate(
            flops=8 * 10**9, bytes_accessed=4 * 10**6, transcendentals=10**6
        ),
        name="edge_part_%d" % part,
    )(
        atom_count, senders.reshape(-1, 128), edge_basis, features, w_recv, w_basis, w_out, *blocks, after
    )


def final_kernel(scale, count_ref, xy_hbm, pos_hbm, factors_ref, *refs):
    parts, (out_ref, xy_ref, pos_ref, arrivals) = refs[:-4], refs[-4:]
    copies = loads((xy_hbm, pos_hbm), (xy_ref, pos_ref), arrivals)
    channels = out_ref.shape[1]
    each = DEVICES // 2
    factors = jnp.concatenate(
        [
            factors_ref[half * each : (half + 1) * each, r * channels : (r + 1) * channels]
            for half in range(2)
            for r in range(ROWS_EACH)
        ],
        axis=0,
    ).T
    total, first = out_ref.shape[0], 0
    for part in parts:
        out_ref[first : first + part.shape[0], :] = part[...]
        first += part.shape[0]
    for copy in copies:
        copy.wait()
    atoms = 256
    for first in range(0, total, atoms):
        flat = flat_waves(xy_ref, pos_ref, first, atoms)
        table = jnp.concatenate(
            [half_table(flat, pos_ref, first, half) for half in range(2)], axis=0
        )
        field = jnp.dot(factors, table, preferred_element_type=jnp.float32)
        live = first + lax.broadcasted_iota(jnp.int32, (atoms, channels), 0) < count_ref[0]
        near = out_ref[first : first + atoms, :]
        out_ref[first : first + atoms, :] = jnp.where(live, near + field.T * scale, 0.0)


def final_call(atom_count, positions, factors, parts, scale):
    atoms = sum(part.shape[0] for part in parts)
    channels = parts[0].shape[1]
    return pl.pallas_call(
        functools.partial(final_kernel, scale),
        in_specs=[pl.BlockSpec(memory_space=pltpu.SMEM), hbm(), hbm(), vmem()]
        + [vmem()] * len(parts),
        out_specs=vmem(),
        out_shape=jax.ShapeDtypeStruct((atoms, channels), jnp.float32),
        scratch_shapes=[
            pltpu.VMEM(XY.shape, jnp.float32),
            pltpu.VMEM(positions.shape, jnp.float32),
            pltpu.SemaphoreType.DMA((2,)),
        ],
        compiler_params=limit(TABLE_VMEM),
        name="updated_rows",
    )(atom_count, jnp.asarray(XY), positions, factors, *parts)


def column_kernel(own_ref, near_ref, beyond_ref, after_ref, out_ref):
    del after_ref
    rows = own_ref.shape[0]
    for at, block in enumerate((own_ref, near_ref, beyond_ref)):
        out_ref[at * rows : (at + 1) * rows, :] = block[...]


def column_call(blocks, after):
    rows, channels = blocks[0].shape
    return pl.pallas_call(
        column_kernel,
        in_specs=[vmem()] * 3 + [pl.BlockSpec(memory_space=pl.ANY)],
        out_specs=vmem(),
        out_shape=jax.ShapeDtypeStruct((3 * rows, channels), blocks[0].dtype),
        compiler_params=limit(SMALL_VMEM),
        name="column_rows",
    )(*blocks, after)


def moved(array, target):
    slabs, subs = lax.axis_size("slab"), lax.axis_size("sub")
    pairs = []
    for s in range(slabs):
        for b in range(subs):
            to_s, to_b = target(s, b)
            pairs.append((s * subs + b, to_s % slabs * subs + to_b % subs))
    return lax.ppermute(array, ("slab", "sub"), pairs)


def to_core(s, b):
    return s ^ 1, b


def to_outer(s, b):
    return s + (1 if s % 2 else -1), b


def to_column(s, b):
    return s, b ^ 1


def to_beyond(s, b):
    return s, b + (-1 if b % 2 == 0 else 1)


def plane_groups(slabs, subs):
    return [
        [
            (z * PLANE + 2 * q + core) * subs + b
            for core in range(2)
            for b in range(subs)
            for q in range(PLANE // 2)
        ]
        for z in range(slabs // PLANE)
    ]


def core_groups(slabs, subs):
    planes = plane_groups(slabs, subs)
    half = len(planes[0]) // 2
    return [group[core * half : (core + 1) * half] for group in planes for core in range(2)]


def line_groups(slabs, subs):
    return [
        [(z * PLANE + q) * subs + b for z in range(slabs // PLANE)]
        for b in range(subs)
        for q in range(PLANE)
    ]


def exchanged(array, groups):
    return lax.all_to_all(array, ("slab", "sub"), 0, 0, axis_index_groups=groups, tiled=True)


def per_device(
    features, positions, atom_count, kgrid, k_filter, w_mix, w_recv, w_send, w_basis, w_out,
    edge_basis, senders,
):
    atoms, channels = features.shape
    total_k = kgrid.shape[1]
    subs, slabs = lax.axis_size("sub"), lax.axis_size("slab")
    packed = prepare_call(atom_count, positions, features)
    other = moved(packed, to_core)
    send_proj = project_call(packed, w_send, atoms, other)
    outer = moved(send_proj, to_outer)
    near = moved(send_proj, to_column)
    beyond = moved(send_proj, to_beyond)
    outer_near = moved(send_proj, lambda s, b: to_outer(*to_column(s, b)))
    outer_beyond = moved(send_proj, lambda s, b: to_outer(*to_beyond(s, b)))

    plane, line = plane_groups(slabs, subs), line_groups(slabs, subs)
    slab = lax.axis_index("slab")
    mine = (slab % 2) * (len(plane[0]) // 2) + lax.axis_index("sub") * (PLANE // 2)
    mine = mine + slab % PLANE // 2
    sums = factor_call(packed, other, atoms)
    core = moved(column_call((send_proj, near, beyond), outer_beyond), to_core)
    blocks = [send_proj, near, beyond, core, outer, outer_near, outer_beyond]
    cores = core_groups(slabs, subs)
    stage_one = stage_call(exchanged(sums, cores), len(cores[0]), len(line[0]))
    count = stage_one.shape[1]
    weights = wave_weights(kgrid, k_filter, mine * count, count)
    norm_factor = 1.0 / math.sqrt(atoms * DEVICES)
    filtered = filter_call(
        exchanged(stage_one, line), weights, w_mix, norm_factor, len(plane[0])
    )
    factors = exchanged(filtered, plane).reshape(DEVICES, -1)

    after = [stage_one, filtered]
    parts = [
        edge_call(p, after[p], atom_count, senders, edge_basis, features, w_recv, w_basis, w_out, blocks)
        for p in range(len(PARTS))
    ]
    return final_call(atom_count, positions, factors, parts, 4.0 / math.sqrt(total_k))


def solution(mesh):
    placed = (
        P(("slab", "sub"), None),
        P(None, ("slab", "sub")),
        P(("slab", "sub")),
        P(), P(), P(), P(), P(), P(), P(),
        P(None, ("slab", "sub")),
        P(("slab", "sub")),
    )
    return jax.shard_map(
        per_device, mesh=mesh, in_specs=placed, out_specs=P(("slab", "sub"), None), check_vma=False
    )
```
